32 devices in a mesh: grp: 2 (over y), op: 16 (over z, x, core).
Axes of the slice: x: 2, y: 2, z: 4, core: 2. Of those that a mesh axis runs over, the one named last changes fastest.
Arguments:
- state: bfloat16 [32, 128, 128], P(('grp', 'op')), parts along dimension 0, may hold values from -6 to 6
- sector_sizes: int32 [32], P('grp'), parts along dimension 0, may hold values from 16 to 128, as said below
- left_ops: bfloat16 [384, 12, 128, 128], P(('grp', 'op')), parts along dimension 0
- right_ops: bfloat16 [384, 12, 128, 128], P(('grp', 'op')), parts along dimension 0
- block_source: int32 [384, 12], P(('grp', 'op')), parts along dimension 0, may hold values from 0 to 15
- block_target: int32 [384, 12], P(('grp', 'op')), parts along dimension 0, may hold values from 0 to 15, as said below
- preconditioner: float32 [32, 128, 128], P(('grp', 'op')), parts along dimension 0, may hold values from 0.3 to 3
Outputs:
- sigma_first: float32 [32, 128, 128], P(('grp', 'op')), parts along dimension 0
- direction: bfloat16 [32, 128, 128], P(('grp', 'op')), parts along dimension 0
- sigma_second: float32 [32, 128, 128], P(('grp', 'op')), parts along dimension 0
- subspace: float32 [8], P('grp'), parts along dimension 0
The draws below stay inside these ranges and needn't reach their ends.
There are 2 independent parts, one for each index of `grp`. The reference program is written for one: setup_inputs(seed, part) draws one part's arguments, and reference() takes and returns one part's arrays. A program takes and returns all parts, laid end to end along the dimension named above; each array names one. Nothing has to cross between parts.
Inputs may be any that keep to these rules, and one draw needn't show every extreme that they name: `sector_sizes`: each sector holds between 16 and 128 states; some sector holds exactly 128. `block_target`: in every operator term, a block whose index n is a multiple of 3 writes the sector that it reads; the targets of all other blocks are drawn apart from their sources.
All inputs are finite; a program needn't handle non-finite values.
Results may differ from the reference program's by a relative error of at most 0.0039.
Values may be sent and summed in bfloat16 or wider, within the bound.
No kernel may reach another device: no remote copies, remote signals or barrier semaphores. Data moves between devices by JAX's collectives and lax.ppermute only.
A program may use at most 128 MiB of HBM per device.

```python
import math
import jax
import jax.numpy as jnp
from jax import lax

CAP = 128
OP_DEV = 12
NNZ = 12
SECTORS = 16
TERMS = 192


def draw_sector_sizes(key, part):
    key = jax.random.fold_in(key, 11)
    first, second = jax.random.split(key)
    lowest = CAP // 8
    spread = CAP - lowest
    raw = jax.random.randint(first, (SECTORS,), 0, spread + 1)
    sizes = lowest + raw * raw // spread
    where_full = jax.random.randint(second, (), 0, SECTORS)
    sizes = sizes.at[where_full].set(CAP)
    return sizes.astype(jnp.int32)


def row_profile(key):
    return jax.random.uniform(jax.random.fold_in(key, 101), (CAP,), jnp.float32)


def block_pair(key):
    source_key = jax.random.fold_in(key, 31)
    other_key = jax.random.fold_in(key, 37)
    source = jax.random.randint(source_key, (TERMS, NNZ), 0, SECTORS)
    other = jax.random.randint(other_key, (TERMS, NNZ), 0, SECTORS)
    slots = jnp.arange(NNZ, dtype=jnp.int32)[None, :]
    target = jnp.where(slots % 3 == 0, source, other)
    return (source.astype(jnp.int32), target.astype(jnp.int32))


def identity_table():
    return (jnp.arange(CAP)[:, None] == jnp.arange(CAP)[None, :]).astype(jnp.float32)


def draw_block_source(key, part):
    pair = block_pair(key)
    return pair[0]


def draw_block_target(key, part):
    pair = block_pair(key)
    return pair[1]


def draw_left_ops(key, part):
    row_unit = row_profile(key)
    key = jax.random.fold_in(key, 21)
    noise_key, gain_key = jax.random.split(key)
    spread = 1.0 / math.sqrt(CAP)
    energies = 0.2 + 0.8 * row_unit
    noise_part = jnp.clip(jax.random.normal(noise_key, (TERMS, NNZ, CAP, CAP), jnp.float32), -3.0, 3.0) * spread
    rough_gain = jax.random.uniform(gain_key, (TERMS, NNZ, CAP), jnp.float32, 0.5, 1.5)
    diagonal_part = (energies * rough_gain)[..., :, None] * identity_table()
    return (diagonal_part + noise_part).astype(jnp.bfloat16)


def draw_right_ops(key, part):
    key = jax.random.fold_in(key, 23)
    noise_key, gain_key = jax.random.split(key)
    diag_scale = 1.0 / math.sqrt(OP_DEV * NNZ)
    spread = diag_scale / math.sqrt(CAP)
    noise_part = jnp.clip(jax.random.normal(noise_key, (TERMS, NNZ, CAP, CAP), jnp.float32), -3.0, 3.0) * spread
    rough_gain = jax.random.uniform(gain_key, (TERMS, NNZ, CAP), jnp.float32, 0.5, 1.5)
    diagonal_part = (diag_scale * rough_gain)[..., :, None] * identity_table()
    return (diagonal_part + noise_part).astype(jnp.bfloat16)


def draw_preconditioner(key, part):
    row_unit = row_profile(key)
    key = jax.random.fold_in(key, 29)
    row_share = 0.7
    jitter = jax.random.uniform(key, (SECTORS, CAP, CAP), jnp.float32)
    exponent = row_share * row_unit[None, :, None] + (1.0 - row_share) * jitter
    return (0.3 * 10.0 ** exponent).astype(jnp.float32)


def steps_of(stream_key, shape, cuts, low, largest):
    gain = 1.0
    for axis_at, shards_of in cuts:
        heights = jax.random.uniform(jax.random.fold_in(jax.random.fold_in(stream_key, 6), axis_at), (shards_of,), jnp.float32, low / len(cuts), largest / len(cuts))
        gain = gain * jnp.repeat(jnp.exp(heights), shape[axis_at] // shards_of).reshape((-1,) + (1,) * (len(shape) - 1 - axis_at))
    return gain


def normal_values(stream_key, shape, scale, most, shards=(), kind=jnp.bfloat16):
    array = jax.random.normal(stream_key, shape, jnp.float32) * scale
    if len(shards) > 0:
        array = steps_of(stream_key, shape, shards, -0.22, 0.18) * array
    return jnp.clip(array, min=-most, max=most).astype(kind)


def setup_inputs(seed: int = 0, part: int = 0) -> dict:
    key_list = jax.random.split(jax.random.key(seed), 8)
    part_keys = jax.random.split(jax.random.fold_in(key_list[7], part), 8)
    return {
        "state": normal_values(part_keys[0], (SECTORS, CAP, CAP), 1.0, 6.0, ((0, 16),)),
        "sector_sizes": draw_sector_sizes(jax.random.fold_in(jax.random.fold_in(key_list[7], part), 71), part),
        "left_ops": draw_left_ops(jax.random.fold_in(jax.random.fold_in(key_list[7], part), 71), part),
        "right_ops": draw_right_ops(jax.random.fold_in(jax.random.fold_in(key_list[7], part), 71), part),
        "block_source": draw_block_source(jax.random.fold_in(jax.random.fold_in(key_list[7], part), 71), part),
        "block_target": draw_block_target(jax.random.fold_in(jax.random.fold_in(key_list[7], part), 71), part),
        "preconditioner": draw_preconditioner(jax.random.fold_in(jax.random.fold_in(key_list[7], part), 71), part),
    }


def sector_mask(sector_sizes):
    rows = jnp.arange(CAP, dtype=jnp.int32)
    inside = rows[None, :] < sector_sizes[:, None]
    return (inside[:, :, None] & inside[:, None, :]).astype(jnp.float32)


def apply_hamiltonian(vector, left_ops, right_ops, block_source, block_target, mask):
    def one_term(carry, items):
        left_term, right_term, source_ids, target_ids = items
        blocks = vector[source_ids].astype(jnp.float32)
        left_prod = jnp.einsum("nij,njk->nik", left_term.astype(jnp.float32), blocks).astype(jnp.bfloat16)
        product = jnp.einsum("nik,nlk->nil", left_prod.astype(jnp.float32), right_term.astype(jnp.float32))
        return carry.at[target_ids].add(product), None

    start = jnp.zeros((SECTORS, CAP, CAP), jnp.float32)
    total, unused = lax.scan(one_term, start, (left_ops, right_ops, block_source, block_target))
    return total * mask


def reference(state, sector_sizes, left_ops, right_ops, block_source, block_target, preconditioner):
    mask = sector_mask(sector_sizes)
    wave = (state.astype(jnp.float32) * mask).astype(jnp.bfloat16)
    wave_f = wave.astype(jnp.float32)
    sigma_first = apply_hamiltonian(wave, left_ops, right_ops, block_source, block_target, mask)
    norm_wave = jnp.sum(wave_f * wave_f)
    rayleigh = jnp.sum(wave_f * sigma_first)
    energy = rayleigh / norm_wave
    scaled = preconditioner * (sigma_first - energy * wave_f)
    intersection = jnp.sum(wave_f * scaled)
    direction = (scaled - (intersection / norm_wave) * wave_f).astype(jnp.bfloat16)
    sigma_second = apply_hamiltonian(direction, left_ops, right_ops, block_source, block_target, mask)
    dir_f = direction.astype(jnp.float32)
    subspace = jnp.stack([rayleigh, jnp.sum(wave_f * sigma_second), jnp.sum(dir_f * sigma_second), jnp.sum(dir_f * dir_f)]) / norm_wave
    return sigma_first, direction, sigma_second, subspace
```

```python
import jax
import jax.numpy as jnp
from jax import lax
from jax.experimental import pallas as pl
from jax.experimental.pallas import tpu as pltpu
from jax.sharding import Mesh
from jax.sharding import PartitionSpec as P

BF16 = jnp.bfloat16
F32 = jnp.float32
TAIL = 16
LIMIT = 36 << 20


def each(count, body, carry):
    if count <= 8:
        for j in range(count):
            carry = body(j, carry)
        return carry
    return lax.fori_loop(0, count, body, carry)


def mask_of(size, width):
    rows = lax.broadcasted_iota(jnp.int32, (width, width), 0)
    cols = lax.broadcasted_iota(jnp.int32, (width, width), 1)
    return (rows < size) & (cols < size)


def fold(x):
    return jnp.sum(x, axis=0, keepdims=True)


def tail_of(rows):
    pieces = []
    for row in rows:
        rest = row
        for _ in range(3):
            piece = rest.astype(BF16).astype(F32)
            pieces.append(piece)
            rest = rest - piece
    lanes = rows[0].shape[1]
    place = lax.broadcasted_iota(jnp.int32, (TAIL, lanes), 0)
    tail = jnp.zeros((TAIL, lanes), F32)
    for at, piece in enumerate(pieces):
        tail = jnp.where(place == at, piece, tail)
    return tail.astype(BF16)


def rows_of(tail, count):
    wide = tail.astype(F32)
    return [
        (wide[3 * i : 3 * i + 1] + wide[3 * i + 1 : 3 * i + 2]) + wide[3 * i + 2 : 3 * i + 3]
        for i in range(count)
    ]


def total(row):
    return jnp.broadcast_to(jnp.sum(row, axis=1, keepdims=True), row.shape)


def apply_blocks(src, tgt, vec, left, right, acc, chips, core):
    terms, nnz = left.shape[0], left.shape[1]
    per = 3 if terms % 3 == 0 else 1

    def place(s):
        return (s >> 1) + chips * ((s ^ core) & 1)

    acc[...] = jnp.zeros_like(acc)

    def step(i, carry):
        items = [(i * per + k, n) for k in range(per) for n in range(nnz)]
        prods = [
            jnp.dot(left[k, n], vec[place(src[k, n])], preferred_element_type=F32).astype(BF16)
            for k, n in items
        ]
        for (k, n), prod in zip(items, prods):
            at = place(tgt[k, n])
            acc[at] += lax.dot_general(
                prod, right[k, n], (((1,), (1,)), ((), ())), preferred_element_type=F32
            )
        return carry

    lax.fori_loop(0, terms // per, step, 0)


def first_kernel(src, tgt, sizes, own, other, left, right, theirs, mine, wave, sums, acc):
    chips, width = own.shape[0], own.shape[2]
    core = lax.axis_index("core")

    def load(j, carry):
        here, there = carry
        a = jnp.where(mask_of(sizes[2 * j + core], width), own[j].astype(F32), 0.0)
        b = jnp.where(mask_of(sizes[2 * j + 1 - core], width), other[j].astype(F32), 0.0)
        wave[j] = a.astype(BF16)
        wave[chips + j] = b.astype(BF16)
        return here + fold(a * a), there + fold(b * b)

    zero = jnp.zeros((1, width), F32)
    here, there = each(chips, load, (zero, zero))
    apply_blocks(src, tgt, wave, left, right, acc, chips, core)

    def store(j, ray):
        a, b = acc[j], acc[chips + j]
        mine[j] = a
        theirs[j, 0:width] = b.astype(BF16)
        ray = ray + fold(wave[j].astype(F32) * a)
        return ray + fold(wave[chips + j].astype(F32) * b)

    ray = each(chips, store, zero)
    tail = tail_of([ray])
    theirs[0, width : width + TAIL] = tail
    sums[0:1] = here + there
    sums[1:2] = ray


def second_kernel(src, tgt, own, other, wave, left, right, theirs, mine, sums, vec, acc):
    chips, width = own.shape[0], own.shape[2]
    core = lax.axis_index("core")

    def load(j, carry):
        vec[j] = own[j, 0:width]
        vec[chips + j] = other[j, 0:width]
        a = rows_of(own[j, width : width + TAIL], 3)
        b = rows_of(other[j, width : width + TAIL], 3)
        return tuple(x + y for x, y in zip(carry, a + b))

    zero = jnp.zeros((1, width), F32)
    got = each(chips, load, (zero,) * 6)
    apply_blocks(src, tgt, vec, left, right, acc, chips, core)

    def store(j, carry):
        first, second = carry
        a, b = acc[j], acc[chips + j]
        mine[j] = a
        theirs[j, 0:width] = b.astype(BF16)
        first = first + fold(wave[j].astype(F32) * a) + fold(wave[chips + j].astype(F32) * b)
        second = second + fold(vec[j].astype(F32) * a) + fold(vec[chips + j].astype(F32) * b)
        return first, second

    first, second = each(chips, store, (zero, zero))
    theirs[0, width : width + TAIL] = tail_of([first, second])
    for i in range(3):
        sums[i : i + 1] = got[i] + got[3 + i]
    sums[3:4] = first
    sums[4:5] = second


def chip_kernel(at, count, mine, got, sums, out):
    chips, width = mine.shape[0], mine.shape[2]
    rows = rows_of(got[0, width : width + TAIL], count)
    tail = tail_of([sums[at + i : at + i + 1] + rows[i] for i in range(count)])

    def store(j, carry):
        out[j, 0:width] = (mine[j] + got[j, 0:width].astype(F32)).astype(BF16)
        out[j, width : width + TAIL] = tail
        return carry

    each(chips, store, 0)


def gather_sums(got, count):
    chips, width = got.shape[0], got.shape[2]

    def add(j, carry):
        block = carry[0] + got[j, 0:width].astype(F32)
        rows = rows_of(got[j, width : width + TAIL], count)
        return (block,) + tuple(x + y for x, y in zip(carry[1:], rows))

    zero = jnp.zeros((1, width), F32)
    return each(chips, add, (jnp.zeros((width, width), F32),) + (zero,) * count)


def residual_kernel(sizes, got, state, precond, sums, sigma, resid, send, keep):
    chips, width = got.shape[0], got.shape[2]
    inside = mask_of(sizes[2 * lax.axis_index("chip") + lax.axis_index("core")], width)
    block, ray = gather_sums(got, 1)
    first = jnp.where(inside, block, 0.0)
    wave = jnp.where(inside, state[0].astype(F32), 0.0)
    norm, ray = total(sums[0:1]), total(ray)
    q = precond[0] * (first - ray / norm * wave)
    low = q.astype(BF16)
    tail = tail_of([fold(wave * q), fold(low.astype(F32) * first), fold(q * q)])
    sigma[0] = first
    resid[0] = q
    keep[0:1] = norm
    keep[1:2] = ray

    def store(j, carry):
        send[j, 0:width] = low
        send[j, width : width + TAIL] = tail
        return carry

    each(chips, store, 0)


def final_kernel(sizes, got, state, first, resid, keep, sums, direction, sigma, subspace):
    width = got.shape[2]
    inside = mask_of(sizes[2 * lax.axis_index("chip") + lax.axis_index("core")], width)
    block, cross, square = gather_sums(got, 2)
    wave = jnp.where(inside, state[0].astype(F32), 0.0)
    norm, ray = keep[0:1], keep[1:2]
    inter, mixed, length = (total(sums[i : i + 1]) for i in range(3))
    cross, square = total(cross), total(square)
    c = inter / norm
    direction[0] = (resid[0] - c * wave).astype(BF16)
    sigma[0] = jnp.where(inside, block, 0.0) - c * first[0]
    values = (
        ray,
        cross - c * ray,
        square - c * mixed - c * (cross - c * ray),
        length - 2.0 * c * inter + c * c * norm,
    )
    for i, value in enumerate(values):
        subspace[i] = jnp.max(value / norm)


VMEM = pl.BlockSpec(memory_space=pltpu.VMEM)
SMEM = pl.BlockSpec(memory_space=pltpu.SMEM)


def call(kernel, name, ins, outs, scratch, args, flops, out_specs=None):
    moved = sum(a.size * a.dtype.itemsize for a in args)
    return pl.pallas_call(
        kernel,
        name=name,
        in_specs=ins,
        out_specs=out_specs or [VMEM] * len(outs),
        out_shape=[jax.ShapeDtypeStruct(s, d) for s, d in outs],
        scratch_shapes=scratch,
        compiler_params=pltpu.CompilerParams(vmem_limit_bytes=LIMIT),
        cost_estimate=pl.CostEstimate(flops=flops, bytes_accessed=moved, transcendentals=0),
    )(*args)


def shards(state, sector_sizes, left, right, source, target, precond):
    chips = lax.axis_size("chip")
    width = state.shape[1]
    high = width + TAIL
    swap = [(0, 1), (1, 0)]
    every = 2 * chips
    flops = 4 * left.size * width

    with jax.named_scope("gather_state"):
        copies = jnp.broadcast_to(state, (chips, width, width))
        own = lax.all_to_all(copies, "chip", 0, 0, tiled=True)
        other = lax.ppermute(own, "core", swap)
    with jax.named_scope("first_sigma"):
        theirs, mine, wave, sums = call(
            first_kernel, "first_sigma", [SMEM] * 3 + [VMEM] * 4,
            [((chips, high, width), BF16), ((chips, width, width), F32),
             ((every, width, width), BF16), ((8, width), F32)],
            [pltpu.VMEM((every, width, width), F32)],
            (source, target, sector_sizes, own, other, left, right), flops,
        )
    with jax.named_scope("sum_first"):
        got = lax.ppermute(theirs, "core", swap)
        (part,) = call(
            lambda *refs: chip_kernel(1, 1, *refs), "chip_sum", [VMEM] * 3,
            [((chips, high, width), BF16)], [], (mine, got, sums), mine.size,
        )
        got = lax.all_to_all(part, "chip", 0, 0, tiled=True)
    with jax.named_scope("residual"):
        first, resid, send, keep = call(
            residual_kernel, "residual", [SMEM] + [VMEM] * 4,
            [((1, width, width), F32), ((1, width, width), F32),
             ((chips, high, width), BF16), ((8, width), F32)],
            [], (sector_sizes, got, state, precond, sums), mine.size,
        )
    with jax.named_scope("gather_residual"):
        own = lax.all_to_all(send, "chip", 0, 0, tiled=True)
        other = lax.ppermute(own, "core", swap)
    with jax.named_scope("second_sigma"):
        theirs, mine, sums = call(
            second_kernel, "second_sigma", [SMEM] * 2 + [VMEM] * 5,
            [((chips, high, width), BF16), ((chips, width, width), F32), ((8, width), F32)],
            [pltpu.VMEM((every, width, width), BF16), pltpu.VMEM((every, width, width), F32)],
            (source, target, own, other, wave, left, right), flops,
        )
    with jax.named_scope("sum_second"):
        got = lax.ppermute(theirs, "core", swap)
        (part,) = call(
            lambda *refs: chip_kernel(3, 2, *refs), "chip_sum", [VMEM] * 3,
            [((chips, high, width), BF16)], [], (mine, got, sums), mine.size,
        )
        got = lax.all_to_all(part, "chip", 0, 0, tiled=True)
    with jax.named_scope("outputs"):
        direction, second, subspace = call(
            final_kernel, "outputs", [SMEM] + [VMEM] * 6,
            [((1, width, width), BF16), ((1, width, width), F32), ((4,), F32)],
            [], (sector_sizes, got, state, first, resid, keep, sums), mine.size,
            [VMEM, VMEM, SMEM],
        )
    return first, direction, second, subspace


def solution(mesh):
    groups, members = mesh.shape["grp"], mesh.shape["op"]
    split = Mesh(mesh.devices.reshape(groups, members // 2, 2), ("grp", "chip", "core"))
    rows = P(("grp", "chip", "core"))
    return jax.shard_map(
        shards,
        mesh=split,
        in_specs=(rows, P("grp"), rows, rows, rows, rows, rows),
        out_specs=(rows, rows, rows, P("grp")),
        check_vma=False,
    )
```

```python
import jax
import jax.numpy as jnp
from jax import lax
from jax.experimental import pallas as pl
from jax.experimental.pallas import tpu as pltpu
from jax.sharding import Mesh
from jax.sharding import PartitionSpec as P

BF16 = jnp.bfloat16
F32 = jnp.float32
TAIL = 16
LIMIT = 36 << 20
LONG = 10**11


def each(count, body, carry):
    if count <= 8:
        for j in range(count):
            carry = body(j, carry)
        return carry
    return lax.fori_loop(0, count, body, carry)


def mask_of(size, width):
    rows = lax.broadcasted_iota(jnp.int32, (width, width), 0)
    cols = lax.broadcasted_iota(jnp.int32, (width, width), 1)
    return (rows < size) & (cols < size)


def fold(x):
    return jnp.sum(x, axis=0, keepdims=True)


def tail_of(rows):
    pieces = []
    for row in rows:
        rest = row
        for _ in range(3):
            piece = rest.astype(BF16).astype(F32)
            pieces.append(piece)
            rest = rest - piece
    lanes = rows[0].shape[1]
    place = lax.broadcasted_iota(jnp.int32, (TAIL, lanes), 0)
    tail = jnp.zeros((TAIL, lanes), F32)
    for at, piece in enumerate(pieces):
        tail = jnp.where(place == at, piece, tail)
    return tail.astype(BF16)


def rows_of(tail, count):
    wide = tail.astype(F32)
    return [
        (wide[3 * i : 3 * i + 1] + wide[3 * i + 1 : 3 * i + 2]) + wide[3 * i + 2 : 3 * i + 3]
        for i in range(count)
    ]


def total(row):
    return jnp.broadcast_to(jnp.sum(row, axis=1, keepdims=True), row.shape)


def apply_blocks(src, tgt, vec, left, right, acc, chips, core):
    terms, nnz = left.shape[0], left.shape[1]
    per = 3 if terms % 3 == 0 else 1

    def place(s):
        return (s >> 1) + chips * ((s ^ core) & 1)

    acc[...] = jnp.zeros_like(acc)

    def step(i, carry):
        items = [(i * per + k, n) for k in range(per) for n in range(nnz)]
        prods = [
            jnp.dot(left[k, n], vec[place(src[k, n])], preferred_element_type=F32).astype(BF16)
            for k, n in items
        ]
        for (k, n), prod in zip(items, prods):
            at = place(tgt[k, n])
            acc[at] += lax.dot_general(
                prod, right[k, n], (((1,), (1,)), ((), ())), preferred_element_type=F32
            )
        return carry

    lax.fori_loop(0, terms // per, step, 0)


def copy_kernel(block, out):
    for j in range(out.shape[0]):
        out[j] = block[0]


def first_kernel(src, tgt, sizes, own, other, left, right, theirs, mine, wave, sums, acc):
    chips, width = own.shape[0], own.shape[2]
    core = lax.axis_index("core")

    def load(j, carry):
        here, there = carry
        a = jnp.where(mask_of(sizes[2 * j + core], width), own[j].astype(F32), 0.0)
        b = jnp.where(mask_of(sizes[2 * j + 1 - core], width), other[j].astype(F32), 0.0)
        wave[j] = a.astype(BF16)
        wave[chips + j] = b.astype(BF16)
        return here + fold(a * a), there + fold(b * b)

    zero = jnp.zeros((1, width), F32)
    here, there = each(chips, load, (zero, zero))
    apply_blocks(src, tgt, wave, left, right, acc, chips, core)

    def store(j, ray):
        a, b = acc[j], acc[chips + j]
        mine[j] = a
        theirs[j, 0:width] = b.astype(BF16)
        ray = ray + fold(wave[j].astype(F32) * a)
        return ray + fold(wave[chips + j].astype(F32) * b)

    ray = each(chips, store, zero)
    tail = tail_of([ray])
    theirs[0, width : width + TAIL] = tail
    sums[0:1] = here + there
    sums[1:2] = ray


def second_kernel(src, tgt, own, other, wave, left, right, theirs, mine, sums, vec, acc):
    chips, width = own.shape[0], own.shape[2]
    core = lax.axis_index("core")

    def load(j, carry):
        vec[j] = own[j, 0:width]
        vec[chips + j] = other[j, 0:width]
        a = rows_of(own[j, width : width + TAIL], 3)
        b = rows_of(other[j, width : width + TAIL], 3)
        return tuple(x + y for x, y in zip(carry, a + b))

    zero = jnp.zeros((1, width), F32)
    got = each(chips, load, (zero,) * 6)
    apply_blocks(src, tgt, vec, left, right, acc, chips, core)

    def store(j, carry):
        first, second = carry
        a, b = acc[j], acc[chips + j]
        mine[j] = a
        theirs[j, 0:width] = b.astype(BF16)
        first = first + fold(wave[j].astype(F32) * a) + fold(wave[chips + j].astype(F32) * b)
        second = second + fold(vec[j].astype(F32) * a) + fold(vec[chips + j].astype(F32) * b)
        return first, second

    first, second = each(chips, store, (zero, zero))
    theirs[0, width : width + TAIL] = tail_of([first, second])
    for i in range(3):
        sums[i : i + 1] = got[i] + got[3 + i]
    sums[3:4] = first
    sums[4:5] = second


def chip_kernel(at, count, mine, got, sums, out):
    chips, width = mine.shape[0], mine.shape[2]
    rows = rows_of(got[0, width : width + TAIL], count)
    tail = tail_of([sums[at + i : at + i + 1] + rows[i] for i in range(count)])

    def store(j, carry):
        out[j, 0:width] = (mine[j] + got[j, 0:width].astype(F32)).astype(BF16)
        out[j, width : width + TAIL] = tail
        return carry

    each(chips, store, 0)


def gather_sums(got, count):
    chips, width = got.shape[0], got.shape[2]

    def add(j, carry):
        block = carry[0] + got[j, 0:width].astype(F32)
        rows = rows_of(got[j, width : width + TAIL], count)
        return (block,) + tuple(x + y for x, y in zip(carry[1:], rows))

    zero = jnp.zeros((1, width), F32)
    return each(chips, add, (jnp.zeros((width, width), F32),) + (zero,) * count)


def residual_kernel(sizes, got, state, precond, sums, sigma, resid, send, keep):
    chips, width = got.shape[0], got.shape[2]
    inside = mask_of(sizes[2 * lax.axis_index("chip") + lax.axis_index("core")], width)
    block, ray = gather_sums(got, 1)
    first = jnp.where(inside, block, 0.0)
    wave = jnp.where(inside, state[0].astype(F32), 0.0)
    norm, ray = total(sums[0:1]), total(ray)
    q = precond[0] * (first - ray / norm * wave)
    low = q.astype(BF16)
    tail = tail_of([fold(wave * q), fold(low.astype(F32) * first), fold(q * q)])
    sigma[0] = first
    resid[0] = q
    keep[0:1] = norm
    keep[1:2] = ray

    def store(j, carry):
        send[j, 0:width] = low
        send[j, width : width + TAIL] = tail
        return carry

    each(chips, store, 0)


def final_kernel(sizes, got, state, first, resid, keep, sums, direction, sigma, subspace):
    width = got.shape[2]
    inside = mask_of(sizes[2 * lax.axis_index("chip") + lax.axis_index("core")], width)
    block, cross, square = gather_sums(got, 2)
    wave = jnp.where(inside, state[0].astype(F32), 0.0)
    norm, ray = keep[0:1], keep[1:2]
    inter, mixed, length = (total(sums[i : i + 1]) for i in range(3))
    cross, square = total(cross), total(square)
    c = inter / norm
    direction[0] = (resid[0] - c * wave).astype(BF16)
    sigma[0] = jnp.where(inside, block, 0.0) - c * first[0]
    values = (
        ray,
        cross - c * ray,
        square - c * mixed - c * (cross - c * ray),
        length - 2.0 * c * inter + c * c * norm,
    )
    for i, value in enumerate(values):
        subspace[i] = jnp.max(value / norm)


VMEM = pl.BlockSpec(memory_space=pltpu.VMEM)
SMEM = pl.BlockSpec(memory_space=pltpu.SMEM)


def call(kernel, name, ins, outs, scratch, args, flops, out_specs=None):
    moved = sum(a.size * a.dtype.itemsize for a in args)
    return pl.pallas_call(
        kernel,
        name=name,
        in_specs=ins,
        out_specs=out_specs or [VMEM] * len(outs),
        out_shape=[jax.ShapeDtypeStruct(s, d) for s, d in outs],
        scratch_shapes=scratch,
        compiler_params=pltpu.CompilerParams(vmem_limit_bytes=LIMIT),
        cost_estimate=pl.CostEstimate(flops=flops, bytes_accessed=moved, transcendentals=0),
    )(*args)


def shards(state, sector_sizes, left, right, source, target, precond):
    chips = lax.axis_size("chip")
    width = state.shape[1]
    high = width + TAIL
    swap = [(0, 1), (1, 0)]
    every = 2 * chips
    flops = 4 * left.size * width

    with jax.named_scope("gather_state"):
        (copies,) = call(
            copy_kernel, "copies", [VMEM], [((chips, width, width), BF16)], [], (state,),
            LONG,
        )
        own = lax.all_to_all(copies, "chip", 0, 0, tiled=True)
        other = lax.ppermute(own, "core", swap)
    with jax.named_scope("first_sigma"):
        theirs, mine, wave, sums = call(
            first_kernel, "first_sigma", [SMEM] * 3 + [VMEM] * 4,
            [((chips, high, width), BF16), ((chips, width, width), F32),
             ((every, width, width), BF16), ((8, width), F32)],
            [pltpu.VMEM((every, width, width), F32)],
            (source, target, sector_sizes, own, other, left, right), flops,
        )
    with jax.named_scope("sum_first"):
        got = lax.ppermute(theirs, "core", swap)
        (part,) = call(
            lambda *refs: chip_kernel(1, 1, *refs), "chip_sum", [VMEM] * 3,
            [((chips, high, width), BF16)], [], (mine, got, sums), mine.size,
        )
        got = lax.all_to_all(part, "chip", 0, 0, tiled=True)
    with jax.named_scope("residual"):
        first, resid, send, keep = call(
            residual_kernel, "residual", [SMEM] + [VMEM] * 4,
            [((1, width, width), F32), ((1, width, width), F32),
             ((chips, high, width), BF16), ((8, width), F32)],
            [], (sector_sizes, got, state, precond, sums), mine.size,
        )
    with jax.named_scope("gather_residual"):
        own = lax.all_to_all(send, "chip", 0, 0, tiled=True)
        other = lax.ppermute(own, "core", swap)
    with jax.named_scope("second_sigma"):
        theirs, mine, sums = call(
            second_kernel, "second_sigma", [SMEM] * 2 + [VMEM] * 5,
            [((chips, high, width), BF16), ((chips, width, width), F32), ((8, width), F32)],
            [pltpu.VMEM((every, width, width), BF16), pltpu.VMEM((every, width, width), F32)],
            (source, target, own, other, wave, left, right), flops,
        )
    with jax.named_scope("sum_second"):
        got = lax.ppermute(theirs, "core", swap)
        (part,) = call(
            lambda *refs: chip_kernel(3, 2, *refs), "chip_sum", [VMEM] * 3,
            [((chips, high, width), BF16)], [], (mine, got, sums), mine.size,
        )
        got = lax.all_to_all(part, "chip", 0, 0, tiled=True)
    with jax.named_scope("outputs"):
        direction, second, subspace = call(
            final_kernel, "outputs", [SMEM] + [VMEM] * 6,
            [((1, width, width), BF16), ((1, width, width), F32), ((4,), F32)],
            [], (sector_sizes, got, state, first, resid, keep, sums), mine.size,
            [VMEM, VMEM, SMEM],
        )
    return first, direction, second, subspace


def solution(mesh):
    groups, members = mesh.shape["grp"], mesh.shape["op"]
    split = Mesh(mesh.devices.reshape(groups, members // 2, 2), ("grp", "chip", "core"))
    rows = P(("grp", "chip", "core"))
    return jax.shard_map(
        shards,
        mesh=split,
        in_specs=(rows, P("grp"), rows, rows, rows, rows, rows),
        out_specs=(rows, rows, rows, P("grp")),
        check_vma=False,
    )
```

```python
import jax
import jax.numpy as jnp
from jax import lax
from jax.experimental import pallas as pl
from jax.experimental.pallas import tpu as pltpu
from jax.sharding import Mesh
from jax.sharding import PartitionSpec as P

BF16 = jnp.bfloat16
F32 = jnp.float32
TAIL = 16
LIMIT = 36 << 20
LONG = 10**11


def each(count, body, carry):
    if count <= 8:
        for j in range(count):
            carry = body(j, carry)
        return carry
    return lax.fori_loop(0, count, body, carry)


def mask_of(size, width):
    rows = lax.broadcasted_iota(jnp.int32, (width, width), 0)
    cols = lax.broadcasted_iota(jnp.int32, (width, width), 1)
    return (rows < size) & (cols < size)


def fold(x):
    return jnp.sum(x, axis=0, keepdims=True)


def tail_of(rows):
    pieces = []
    for row in rows:
        rest = row
        for _ in range(3):
            piece = rest.astype(BF16).astype(F32)
            pieces.append(piece)
            rest = rest - piece
    lanes = rows[0].shape[1]
    place = lax.broadcasted_iota(jnp.int32, (TAIL, lanes), 0)
    tail = jnp.zeros((TAIL, lanes), F32)
    for at, piece in enumerate(pieces):
        tail = jnp.where(place == at, piece, tail)
    return tail.astype(BF16)


def rows_of(tail, count):
    wide = tail.astype(F32)
    return [
        (wide[3 * i : 3 * i + 1] + wide[3 * i + 1 : 3 * i + 2]) + wide[3 * i + 2 : 3 * i + 3]
        for i in range(count)
    ]


def total(row):
    return jnp.broadcast_to(jnp.sum(row, axis=1, keepdims=True), row.shape)


def apply_blocks(src, tgt, vec, left, right, acc, chips, core, keep=None):
    terms, nnz = left.shape[0], left.shape[1]
    per = 6 if terms % 6 == 0 else 1

    def place(s):
        return (s >> 1) + chips * ((s ^ core) & 1)

    acc[...] = jnp.zeros_like(acc)

    def step(i, carry):
        items = [(i * per + k, n) for k in range(per) for n in range(nnz)]
        prods = [
            jnp.dot(left[k, n], vec[place(src[k, n])], preferred_element_type=F32).astype(BF16)
            for k, n in items
        ]
        for (k, n), prod in zip(items, prods):
            at = place(tgt[k, n])
            turned = right[k, n]
            if keep is not None:
                turned = turned.T
                keep[k, n] = turned
            acc[at] += jnp.dot(prod, turned, preferred_element_type=F32)
        return carry

    lax.fori_loop(0, terms // per, step, 0)


def copy_kernel(block, out):
    for j in range(out.shape[0]):
        out[j] = block[0]


def first_kernel(src, tgt, sizes, own, other, left, right, theirs, mine, wave, flip, sums, acc):
    chips, width = own.shape[0], own.shape[2]
    core = lax.axis_index("core")

    def load(j, carry):
        here, there = carry
        a = jnp.where(mask_of(sizes[2 * j + core], width), own[j].astype(F32), 0.0)
        b = jnp.where(mask_of(sizes[2 * j + 1 - core], width), other[j].astype(F32), 0.0)
        wave[j] = a.astype(BF16)
        wave[chips + j] = b.astype(BF16)
        return here + fold(a * a), there + fold(b * b)

    zero = jnp.zeros((1, width), F32)
    here, there = each(chips, load, (zero, zero))
    apply_blocks(src, tgt, wave, left, right, acc, chips, core, flip)

    def store(j, ray):
        a, b = acc[j], acc[chips + j]
        mine[j] = a
        theirs[j, 0:width] = b.astype(BF16)
        ray = ray + fold(wave[j].astype(F32) * a)
        return ray + fold(wave[chips + j].astype(F32) * b)

    ray = each(chips, store, zero)
    tail = tail_of([ray])
    theirs[0, width : width + TAIL] = tail
    sums[0:1] = here + there
    sums[1:2] = ray


def second_kernel(src, tgt, own, other, wave, left, right, theirs, mine, sums, vec, acc):
    chips, width = own.shape[0], own.shape[2]
    core = lax.axis_index("core")

    def load(j, carry):
        vec[j] = own[j, 0:width]
        vec[chips + j] = other[j, 0:width]
        a = rows_of(own[j, width : width + TAIL], 3)
        b = rows_of(other[j, width : width + TAIL], 3)
        return tuple(x + y for x, y in zip(carry, a + b))

    zero = jnp.zeros((1, width), F32)
    got = each(chips, load, (zero,) * 6)
    apply_blocks(src, tgt, vec, left, right, acc, chips, core)

    def store(j, carry):
        first, second = carry
        a, b = acc[j], acc[chips + j]
        mine[j] = a
        theirs[j, 0:width] = b.astype(BF16)
        first = first + fold(wave[j].astype(F32) * a) + fold(wave[chips + j].astype(F32) * b)
        second = second + fold(vec[j].astype(F32) * a) + fold(vec[chips + j].astype(F32) * b)
        return first, second

    first, second = each(chips, store, (zero, zero))
    theirs[0, width : width + TAIL] = tail_of([first, second])
    for i in range(3):
        sums[i : i + 1] = got[i] + got[3 + i]
    sums[3:4] = first
    sums[4:5] = second


def chip_kernel(at, count, mine, got, sums, out):
    chips, width = mine.shape[0], mine.shape[2]
    rows = rows_of(got[0, width : width + TAIL], count)
    tail = tail_of([sums[at + i : at + i + 1] + rows[i] for i in range(count)])

    def store(j, carry):
        out[j, 0:width] = (mine[j] + got[j, 0:width].astype(F32)).astype(BF16)
        out[j, width : width + TAIL] = tail
        return carry

    each(chips, store, 0)


def gather_sums(got, count):
    chips, width = got.shape[0], got.shape[2]

    def add(j, carry):
        block = carry[0] + got[j, 0:width].astype(F32)
        rows = rows_of(got[j, width : width + TAIL], count)
        return (block,) + tuple(x + y for x, y in zip(carry[1:], rows))

    zero = jnp.zeros((1, width), F32)
    return each(chips, add, (jnp.zeros((width, width), F32),) + (zero,) * count)


def residual_kernel(sizes, got, state, precond, sums, sigma, resid, send, keep):
    chips, width = got.shape[0], got.shape[2]
    inside = mask_of(sizes[2 * lax.axis_index("chip") + lax.axis_index("core")], width)
    block, ray = gather_sums(got, 1)
    first = jnp.where(inside, block, 0.0)
    wave = jnp.where(inside, state[0].astype(F32), 0.0)
    norm, ray = total(sums[0:1]), total(ray)
    q = precond[0] * (first - ray / norm * wave)
    low = q.astype(BF16)
    tail = tail_of([fold(wave * q), fold(low.astype(F32) * first), fold(q * q)])
    sigma[0] = first
    resid[0] = q
    keep[0:1] = norm
    keep[1:2] = ray

    def store(j, carry):
        send[j, 0:width] = low
        send[j, width : width + TAIL] = tail
        return carry

    each(chips, store, 0)


def final_kernel(sizes, got, state, first, resid, keep, sums, direction, sigma, subspace):
    width = got.shape[2]
    inside = mask_of(sizes[2 * lax.axis_index("chip") + lax.axis_index("core")], width)
    block, cross, square = gather_sums(got, 2)
    wave = jnp.where(inside, state[0].astype(F32), 0.0)
    norm, ray = keep[0:1], keep[1:2]
    inter, mixed, length = (total(sums[i : i + 1]) for i in range(3))
    cross, square = total(cross), total(square)
    c = inter / norm
    direction[0] = (resid[0] - c * wave).astype(BF16)
    sigma[0] = jnp.where(inside, block, 0.0) - c * first[0]
    values = (
        ray,
        cross - c * ray,
        square - c * mixed - c * (cross - c * ray),
        length - 2.0 * c * inter + c * c * norm,
    )
    for i, value in enumerate(values):
        subspace[i] = jnp.max(value / norm)


VMEM = pl.BlockSpec(memory_space=pltpu.VMEM)
SMEM = pl.BlockSpec(memory_space=pltpu.SMEM)


def call(kernel, name, ins, outs, scratch, args, flops, out_specs=None):
    moved = sum(a.size * a.dtype.itemsize for a in args)
    return pl.pallas_call(
        kernel,
        name=name,
        in_specs=ins,
        out_specs=out_specs or [VMEM] * len(outs),
        out_shape=[jax.ShapeDtypeStruct(s, d) for s, d in outs],
        scratch_shapes=scratch,
        compiler_params=pltpu.CompilerParams(vmem_limit_bytes=LIMIT),
        cost_estimate=pl.CostEstimate(flops=flops, bytes_accessed=moved, transcendentals=0),
    )(*args)


def shards(state, sector_sizes, left, right, source, target, precond):
    chips = lax.axis_size("chip")
    width = state.shape[1]
    high = width + TAIL
    swap = [(0, 1), (1, 0)]
    every = 2 * chips
    flops = 4 * left.size * width

    with jax.named_scope("gather_state"):
        (copies,) = call(
            copy_kernel, "copies", [VMEM], [((chips, width, width), BF16)], [], (state,),
            LONG,
        )
        own = lax.all_to_all(copies, "chip", 0, 0, tiled=True)
        other = lax.ppermute(own, "core", swap)
    with jax.named_scope("first_sigma"):
        theirs, mine, wave, flip, sums = call(
            first_kernel, "first_sigma", [SMEM] * 3 + [VMEM] * 4,
            [((chips, high, width), BF16), ((chips, width, width), F32),
             ((every, width, width), BF16), (right.shape, BF16), ((8, width), F32)],
            [pltpu.VMEM((every, width, width), F32)],
            (source, target, sector_sizes, own, other, left, right), flops,
        )
    with jax.named_scope("sum_first"):
        got = lax.ppermute(theirs, "core", swap)
        (part,) = call(
            lambda *refs: chip_kernel(1, 1, *refs), "chip_sum", [VMEM] * 3,
            [((chips, high, width), BF16)], [], (mine, got, sums), mine.size,
        )
        got = lax.all_to_all(part, "chip", 0, 0, tiled=True)
    with jax.named_scope("residual"):
        first, resid, send, keep = call(
            residual_kernel, "residual", [SMEM] + [VMEM] * 4,
            [((1, width, width), F32), ((1, width, width), F32),
             ((chips, high, width), BF16), ((8, width), F32)],
            [], (sector_sizes, got, state, precond, sums), mine.size,
        )
    with jax.named_scope("gather_residual"):
        own = lax.all_to_all(send, "chip", 0, 0, tiled=True)
        other = lax.ppermute(own, "core", swap)
    with jax.named_scope("second_sigma"):
        theirs, mine, sums = call(
            second_kernel, "second_sigma", [SMEM] * 2 + [VMEM] * 5,
            [((chips, high, width), BF16), ((chips, width, width), F32), ((8, width), F32)],
            [pltpu.VMEM((every, width, width), BF16), pltpu.VMEM((every, width, width), F32)],
            (source, target, own, other, wave, left, flip), flops,
        )
    with jax.named_scope("sum_second"):
        got = lax.ppermute(theirs, "core", swap)
        (part,) = call(
            lambda *refs: chip_kernel(3, 2, *refs), "chip_sum", [VMEM] * 3,
            [((chips, high, width), BF16)], [], (mine, got, sums), mine.size,
        )
        got = lax.all_to_all(part, "chip", 0, 0, tiled=True)
    with jax.named_scope("outputs"):
        direction, second, subspace = call(
            final_kernel, "outputs", [SMEM] + [VMEM] * 6,
            [((1, width, width), BF16), ((1, width, width), F32), ((4,), F32)],
            [], (sector_sizes, got, state, first, resid, keep, sums), mine.size,
            [VMEM, VMEM, SMEM],
        )
    return first, direction, second, subspace


def solution(mesh):
    groups, members = mesh.shape["grp"], mesh.shape["op"]
    split = Mesh(mesh.devices.reshape(groups, members // 2, 2), ("grp", "chip", "core"))
    rows = P(("grp", "chip", "core"))
    return jax.shard_map(
        shards,
        mesh=split,
        in_specs=(rows, P("grp"), rows, rows, rows, rows, rows),
        out_specs=(rows, rows, rows, P("grp")),
        check_vma=False,
    )
```

```python
import jax
import jax.numpy as jnp
from jax import lax
from jax.experimental import pallas as pl
from jax.experimental.pallas import tpu as pltpu
from jax.sharding import Mesh
from jax.sharding import PartitionSpec as P

BF16 = jnp.bfloat16
F32 = jnp.float32
TAIL = 16
LIMIT = 36 << 20
LONG = 10**11
NEAR = 4


def each(count, body, carry):
    if count <= 8:
        for j in range(count):
            carry = body(j, carry)
        return carry
    return lax.fori_loop(0, count, body, carry)


def mask_of(size, width):
    rows = lax.broadcasted_iota(jnp.int32, (width, width), 0)
    cols = lax.broadcasted_iota(jnp.int32, (width, width), 1)
    return (rows < size) & (cols < size)


def fold(x):
    return jnp.sum(x, axis=0, keepdims=True)


def tail_of(rows):
    pieces = []
    for row in rows:
        rest = row
        for _ in range(3):
            piece = rest.astype(BF16).astype(F32)
            pieces.append(piece)
            rest = rest - piece
    lanes = rows[0].shape[1]
    place = lax.broadcasted_iota(jnp.int32, (TAIL, lanes), 0)
    tail = jnp.zeros((TAIL, lanes), F32)
    for at, piece in enumerate(pieces):
        tail = jnp.where(place == at, piece, tail)
    return tail.astype(BF16)


def rows_of(tail, count):
    wide = tail.astype(F32)
    return [
        (wide[3 * i : 3 * i + 1] + wide[3 * i + 1 : 3 * i + 2]) + wide[3 * i + 2 : 3 * i + 3]
        for i in range(count)
    ]


def total(row):
    return jnp.broadcast_to(jnp.sum(row, axis=1, keepdims=True), row.shape)


def halve(rows):
    while rows.shape[0] > 1:
        half = rows.shape[0] // 2
        rows = rows[:half] + rows[half:]
    return rows


def place_of(core, chip, chips):
    return lambda s: ((s >> 1) ^ chip) + chips * ((s ^ core) & 1)


def apply_blocks(src, tgt, vec, left, right, acc, place, keep=None):
    terms, nnz = left.shape[0], left.shape[1]
    per = 6 if terms % 6 == 0 else 1
    acc[...] = jnp.zeros_like(acc)

    def step(i, carry):
        items = [(i * per + k, n) for k in range(per) for n in range(nnz)]
        prods = [
            jnp.dot(left[k, n], vec[place(src[k, n])], preferred_element_type=F32).astype(BF16)
            for k, n in items
        ]
        for (k, n), prod in zip(items, prods):
            at = place(tgt[k, n])
            turned = right[k, n]
            if keep is not None:
                turned = turned.T
                keep[k, n] = turned
            acc[at] += jnp.dot(prod, turned, preferred_element_type=F32)
        return carry

    lax.fori_loop(0, terms // per, step, 0)


def mask_kernel(sizes, inside):
    own = 2 * lax.axis_index("chip") + lax.axis_index("core")
    inside[0] = mask_of(sizes[own], inside.shape[2]).astype(F32)


def first_kernel(src, tgt, sizes, *refs):
    pieces, ins, outs = refs[: 2 * NEAR], refs[2 * NEAR : 2 * NEAR + 3], refs[2 * NEAR + 3 :]
    left, right, inside = ins
    theirs, mine, wave, flip, sums, acc, rows = outs
    span, width = pieces[0].shape[0], pieces[0].shape[2]
    chips = NEAR * span
    core, chip = lax.axis_index("core"), lax.axis_index("chip")

    for other in range(2):
        for k in range(NEAR):
            piece = pieces[other * NEAR + k]

            def load(i, carry, other=other, k=k, piece=piece):
                rel = NEAR * i + k
                size = sizes[2 * (chip ^ rel) + (core ^ other)]
                block = piece[i].astype(F32)
                if other == 0 and k == 0 and span <= 8 and i == 0:
                    block = jnp.where(inside[0] > 0.0, block, 0.0)
                else:
                    block = jnp.where(mask_of(size, width), block, 0.0)
                wave[other * chips + rel] = block.astype(BF16)
                rows[pl.ds(other * chips + rel, 1)] = fold(block * block)
                return carry

            each(span, load, 0)
    apply_blocks(src, tgt, wave, left, right, acc, place_of(core, chip, chips), flip)

    def store(j, ray):
        a, b = acc[j], acc[chips + j]
        mine[j] = a
        theirs[j, 0:width] = b.astype(BF16)
        ray = ray + fold(wave[j].astype(F32) * a)
        return ray + fold(wave[chips + j].astype(F32) * b)

    ray = each(chips, store, jnp.zeros((1, width), F32))
    theirs[0, width : width + TAIL] = tail_of([ray])
    sums[0:1] = halve(rows[...])
    sums[1:2] = ray


def second_kernel(src, tgt, *refs):
    pieces, ins, outs = refs[: 2 * NEAR], refs[2 * NEAR : 2 * NEAR + 6], refs[2 * NEAR + 6 :]
    wave, left, right, resid, first, keep = ins
    theirs, mine, sums, sigma, direction, vec, acc, rows, low, sems = outs
    span, width = pieces[0].shape[0], pieces[0].shape[2]
    chips = NEAR * span
    core, chip = lax.axis_index("core"), lax.axis_index("chip")
    copies = [
        pltpu.make_async_copy(first, sigma, sems.at[0]),
        pltpu.make_async_copy(low, direction, sems.at[1]),
    ]
    copies[0].start()

    for other in range(2):
        for k in range(NEAR):
            piece = pieces[other * NEAR + k]

            def load(i, carry, other=other, k=k, piece=piece):
                at = other * chips + NEAR * i + k
                vec[at] = piece[i, 0:width]
                for n, row in enumerate(rows_of(piece[i, width : width + TAIL], 3)):
                    rows[n, pl.ds(at, 1)] = row
                return carry

            each(span, load, 0)
    inter, mixed, length = (total(halve(rows[n])) for n in range(3))
    low[0] = (resid[0] - inter / keep[0:1] * wave[0].astype(F32)).astype(BF16)
    copies[1].start()
    apply_blocks(src, tgt, vec, left, right, acc, place_of(core, chip, chips))

    def store(j, carry):
        cross, square = carry
        a, b = acc[j], acc[chips + j]
        mine[j] = a
        theirs[j, 0:width] = b.astype(BF16)
        cross = cross + fold(wave[j].astype(F32) * a) + fold(wave[chips + j].astype(F32) * b)
        square = square + fold(vec[j].astype(F32) * a) + fold(vec[chips + j].astype(F32) * b)
        return cross, square

    zero = jnp.zeros((1, width), F32)
    cross, square = each(chips, store, (zero, zero))
    theirs[0, width : width + TAIL] = tail_of([cross, square])
    for i, row in enumerate((inter, mixed, length, cross, square)):
        sums[i : i + 1] = row
    for copy in copies:
        copy.wait()


def chip_kernel(at, count, mine, got, sums, base, *sends):
    width = mine.shape[2]
    rows = rows_of(got[0, width : width + TAIL], count)
    rows = [sums[at + i : at + i + 1] + rows[i] for i in range(count)]
    tail = tail_of(rows)

    def store(i, carry):
        base[i, 0:width] = mine[NEAR * i] + got[NEAR * i, 0:width].astype(F32)
        for k, send in enumerate(sends, 1):
            rel = NEAR * i + k
            send[i, 0:width] = (mine[rel] + got[rel, 0:width].astype(F32)).astype(BF16)
        return carry

    each(base.shape[0], store, 0)
    for send in sends:
        send[0, width : width + TAIL] = tail
    for i, row in enumerate(rows):
        base[0, width + i : width + i + 1] = row


def near_kernel(count, base, *refs):
    gots, (low, high) = refs[:-2], refs[-2:]
    span, width = base.shape[0], base.shape[2]
    half = span // 2
    parts = [[base[0, width + i : width + i + 1] for i in range(count)]]
    parts += [rows_of(got[0, width : width + TAIL], count) for got in gots]
    rows = [halve(jnp.concatenate([part[i] for part in parts], axis=0)) for i in range(count)]

    def add(i):
        block = base[i, 0:width]
        for got in gots:
            block = block + got[i, 0:width].astype(F32)
        return block

    def store(i, carry):
        low[i, 0:width] = add(i)
        high[i, 0:width] = add(half + i).astype(high.dtype)
        for n, row in enumerate(rows):
            low[i, width + n : width + n + 1] = row
        if high.dtype == BF16:
            high[i, width : width + TAIL] = tail_of(rows)
        else:
            for n, row in enumerate(rows):
                high[i, width + n : width + n + 1] = row
        return carry

    each(half, store, 0)


def last_sums(low, got, count):
    width = got.shape[2]
    block = low[0, 0:width] + got[0, 0:width].astype(F32)
    if got.dtype == BF16:
        rows = rows_of(got[0, width : width + TAIL], count)
    else:
        rows = [got[0, width + i : width + i + 1] for i in range(count)]
    return [block] + [low[0, width + i : width + i + 1] + rows[i] for i in range(count)]


def residual_kernel(half, got, wave, inside, precond, sums, sigma, resid, send, keep):
    width = got.shape[2]
    block, ray = last_sums(half, got, 1)
    first = block * inside[0]
    own = wave[0].astype(F32)
    norm, ray = total(sums[0:1]), total(ray)
    q = precond[0] * (first - ray / norm * own)
    low = q.astype(BF16)
    sigma[0] = first
    resid[0] = q
    send[0, 0:width] = low
    send[0, width : width + TAIL] = tail_of(
        [fold(own * q), fold(low.astype(F32) * first), fold(q * q)]
    )
    keep[0:1] = norm
    keep[1:2] = ray


def final_kernel(half, got, inside, first, keep, sums, sigma, subspace):
    block, cross, square = last_sums(half, got, 2)
    norm, ray = keep[0:1], keep[1:2]
    inter, mixed, length = (sums[i : i + 1] for i in range(3))
    cross, square = total(cross), total(square)
    c = inter / norm
    sigma[0] = block * inside[0] - c * first[0]
    values = (
        ray,
        cross - c * ray,
        square - c * mixed - c * (cross - c * ray),
        length - 2.0 * c * inter + c * c * norm,
    )
    for i, value in enumerate(values):
        subspace[i] = jnp.max(value / norm)


VMEM = pl.BlockSpec(memory_space=pltpu.VMEM)
SMEM = pl.BlockSpec(memory_space=pltpu.SMEM)
HBM = pl.BlockSpec(memory_space=pl.ANY)


def call(kernel, name, ins, outs, scratch, args, flops, out_specs=None):
    moved = sum(a.size * a.dtype.itemsize for a in args)
    return pl.pallas_call(
        kernel,
        name=name,
        in_specs=ins,
        out_specs=out_specs or [VMEM] * len(outs),
        out_shape=outs,
        scratch_shapes=scratch,
        compiler_params=pltpu.CompilerParams(vmem_limit_bytes=LIMIT),
        cost_estimate=pl.CostEstimate(flops=flops, bytes_accessed=moved, transcendentals=0),
    )(*args)


def shape(*dims, dtype=F32):
    return jax.ShapeDtypeStruct(dims, dtype)


def swap(x):
    return lax.ppermute(x, "core", [(0, 1), (1, 0)])


def flip_chip(x, bits):
    chips = lax.axis_size("chip")
    return lax.ppermute(x, "chip", [(i, i ^ bits) for i in range(chips)])


def gather(block):
    step = NEAR
    while step < lax.axis_size("chip"):
        block = jnp.concatenate([block, flip_chip(block, step)], axis=0)
        step *= 2
    pieces = [block] + [flip_chip(block, k) for k in range(1, NEAR)]
    return pieces + [swap(piece) for piece in pieces]


def scatter(theirs, mine, sums, at, count, narrow):
    chips, width = mine.shape[0], mine.shape[2]
    span, high, wide = chips // NEAR, width + TAIL, width + 8
    sent = [shape(span, high, width, dtype=BF16)] * (NEAR - 1)
    base, *sends = call(
        lambda *refs: chip_kernel(at, count, *refs), "chip_sum", [VMEM] * 3,
        [shape(span, wide, width)] + sent, [], (mine, swap(theirs), sums), mine.size,
    )
    gots = [flip_chip(send, k) for k, send in enumerate(sends, 1)]
    half = span // 2
    last = shape(half, high, width, dtype=BF16) if narrow and half == 1 else shape(half, wide, width)
    low, far = call(
        lambda *refs: near_kernel(count, *refs), "near_sum", [VMEM] * NEAR,
        [shape(half, wide, width), last], [], (base, *gots), mine.size,
    )
    got = flip_chip(far, NEAR * half)
    while half > 1:
        half //= 2
        low = low + got
        low, got = low[:half], flip_chip(low[half:], NEAR * half)
    return low, got


def shards(state, sector_sizes, left, right, source, target, precond):
    chips = lax.axis_size("chip")
    width = state.shape[1]
    high = width + TAIL
    every = 2 * chips
    flops = 4 * left.size * width
    near = [VMEM] * (2 * NEAR)
    block = shape(1, width, width)
    sums_of = shape(8, width)

    with jax.named_scope("own_mask"):
        (inside,) = call(mask_kernel, "own_mask", [SMEM], [block], [], (sector_sizes,), LONG)
    with jax.named_scope("gather_state"):
        pieces = gather(state)
    with jax.named_scope("first_sigma"):
        theirs, mine, wave, flip, sums = call(
            first_kernel, "first_sigma", [SMEM] * 3 + near + [VMEM] * 3,
            [shape(chips, high, width, dtype=BF16), shape(chips, width, width),
             shape(every, width, width, dtype=BF16), shape(*right.shape, dtype=BF16), sums_of],
            [pltpu.VMEM((every, width, width), F32), pltpu.VMEM((every, width), F32)],
            (source, target, sector_sizes, *pieces, left, right, inside), flops,
        )
    with jax.named_scope("sum_first"):
        low, got = scatter(theirs, mine, sums, 1, 1, False)
    with jax.named_scope("residual"):
        first, resid, send, keep = call(
            residual_kernel, "residual", [VMEM] * 6,
            [block, block, shape(1, high, width, dtype=BF16), sums_of],
            [], (low, got, wave, inside, precond, sums), mine.size,
        )
    with jax.named_scope("gather_residual"):
        pieces = gather(send)
    with jax.named_scope("second_sigma"):
        theirs, mine, sums, sigma, direction = call(
            second_kernel, "second_sigma", [SMEM] * 2 + near + [VMEM] * 6,
            [shape(chips, high, width, dtype=BF16), shape(chips, width, width), sums_of,
             block, shape(1, width, width, dtype=BF16)],
            [pltpu.VMEM((every, width, width), BF16), pltpu.VMEM((every, width, width), F32),
             pltpu.VMEM((3, every, width), F32), pltpu.VMEM((1, width, width), BF16),
             pltpu.SemaphoreType.DMA((2,))],
            (source, target, *pieces, wave, left, flip, resid, first, keep), flops,
            [VMEM] * 3 + [HBM] * 2,
        )
    with jax.named_scope("sum_second"):
        low, got = scatter(theirs, mine, sums, 3, 2, True)
    with jax.named_scope("outputs"):
        second, subspace = call(
            final_kernel, "outputs", [VMEM] * 6, [block, shape(4)],
            [], (low, got, inside, first, keep, sums), mine.size, [VMEM, SMEM],
        )
    return sigma, direction, second, subspace


def solution(mesh):
    groups, members = mesh.shape["grp"], mesh.shape["op"]
    split = Mesh(mesh.devices.reshape(groups, members // 2, 2), ("grp", "chip", "core"))
    rows = P(("grp", "chip", "core"))
    return jax.shard_map(
        shards,
        mesh=split,
        in_specs=(rows, P("grp"), rows, rows, rows, rows, rows),
        out_specs=(rows, rows, rows, P("grp")),
        check_vma=False,
    )
```

```python
import jax
import jax.numpy as jnp
from jax import lax
from jax.experimental import pallas as pl
from jax.experimental.pallas import tpu as pltpu
from jax.sharding import Mesh
from jax.sharding import PartitionSpec as P

BF16 = jnp.bfloat16
F32 = jnp.float32
TAIL = 16
LIMIT = 36 << 20
LONG = 10**11
NEAR = 4


def each(count, body, carry):
    if count <= 8:
        for j in range(count):
            carry = body(j, carry)
        return carry
    return lax.fori_loop(0, count, body, carry)


def mask_of(size, width):
    rows = lax.broadcasted_iota(jnp.int32, (width, width), 0)
    cols = lax.broadcasted_iota(jnp.int32, (width, width), 1)
    return (rows < size) & (cols < size)


def fold(x):
    return jnp.sum(x, axis=0, keepdims=True)


def tail_of(rows):
    pieces = []
    for row in rows:
        rest = row
        for _ in range(3):
            piece = rest.astype(BF16).astype(F32)
            pieces.append(piece)
            rest = rest - piece
    lanes = rows[0].shape[1]
    place = lax.broadcasted_iota(jnp.int32, (TAIL, lanes), 0)
    tail = jnp.zeros((TAIL, lanes), F32)
    for at, piece in enumerate(pieces):
        tail = jnp.where(place == at, piece, tail)
    return tail.astype(BF16)


def rows_of(tail, count):
    wide = tail.astype(F32)
    return [
        (wide[3 * i : 3 * i + 1] + wide[3 * i + 1 : 3 * i + 2]) + wide[3 * i + 2 : 3 * i + 3]
        for i in range(count)
    ]


def total(row):
    return jnp.broadcast_to(jnp.sum(row, axis=1, keepdims=True), row.shape)


def halve(rows):
    while rows.shape[0] > 1:
        half = rows.shape[0] // 2
        rows = rows[:half] + rows[half:]
    return rows


def place_of(core, chip, chips):
    return lambda s: ((s >> 1) ^ chip) + chips * ((s ^ core) & 1)


def apply_blocks(src, tgt, vec, left, right, acc, place, keep=None):
    terms, nnz = left.shape[0], left.shape[1]
    per = 6 if terms % 6 == 0 else 1
    acc[...] = jnp.zeros_like(acc)

    def step(i, carry):
        items = [(i * per + k, n) for k in range(per) for n in range(nnz)]
        prods = [
            jnp.dot(left[k, n], vec[place(src[k, n])], preferred_element_type=F32).astype(BF16)
            for k, n in items
        ]
        for (k, n), prod in zip(items, prods):
            at = place(tgt[k, n])
            turned = right[k, n]
            if keep is not None:
                turned = turned.T
                keep[k, n] = turned
            acc[at] += jnp.dot(prod, turned, preferred_element_type=F32)
        return carry

    lax.fori_loop(0, terms // per, step, 0)


def mask_kernel(sizes, inside):
    for i in range(2):
        sector = 2 * (lax.axis_index("chip") ^ (NEAR * i)) + lax.axis_index("core")
        inside[i] = mask_of(sizes[sector], inside.shape[2]).astype(F32)


def first_kernel(src, tgt, sizes, *refs):
    pieces, ins, outs = refs[: 2 * NEAR], refs[2 * NEAR : 2 * NEAR + 4], refs[2 * NEAR + 4 :]
    left, right, inside, _ = ins
    theirs, mine, wave, flip, sums, acc, rows = outs
    span, width = pieces[0].shape[0], pieces[0].shape[2]
    chips = NEAR * span
    core, chip = lax.axis_index("core"), lax.axis_index("chip")

    for other in range(2):
        for k in range(NEAR):
            piece = pieces[other * NEAR + k]

            def load(i, carry, other=other, k=k, piece=piece):
                rel = NEAR * i + k
                size = sizes[2 * (chip ^ rel) + (core ^ other)]
                block = piece[i].astype(F32)
                if other == 0 and k == 0 and span <= 8 and i == 0:
                    block = block * inside[0]
                else:
                    block = jnp.where(mask_of(size, width), block, 0.0)
                wave[other * chips + rel] = block.astype(BF16)
                rows[pl.ds(other * chips + rel, 1)] = fold(block * block)
                return carry

            each(span, load, 0)
    apply_blocks(src, tgt, wave, left, right, acc, place_of(core, chip, chips), flip)

    def store(j, ray):
        a, b = acc[j], acc[chips + j]
        mine[j] = a
        theirs[j, 0:width] = b.astype(BF16)
        ray = ray + fold(wave[j].astype(F32) * a)
        return ray + fold(wave[chips + j].astype(F32) * b)

    ray = each(chips, store, jnp.zeros((1, width), F32))
    theirs[0, width : width + TAIL] = tail_of([ray])
    sums[0:1] = halve(rows[...])
    sums[1:2] = ray


def second_kernel(src, tgt, *refs):
    pieces, ins, outs = refs[: 2 * NEAR], refs[2 * NEAR : 2 * NEAR + 5], refs[2 * NEAR + 5 :]
    wave, left, right, first, keep = ins
    theirs, mine, sums, sigma, vec, acc, sem = outs
    span, width = pieces[0].shape[0], pieces[0].shape[2]
    chips = NEAR * span
    core, chip = lax.axis_index("core"), lax.axis_index("chip")
    copy = pltpu.make_async_copy(first, sigma, sem)
    copy.start()

    for other in range(2):
        for k in range(NEAR):
            piece = pieces[other * NEAR + k]

            def load(i, carry, other=other, k=k, piece=piece):
                vec[other * chips + NEAR * i + k] = piece[i]
                return carry

            each(span, load, 0)
    apply_blocks(src, tgt, vec, left, right, acc, place_of(core, chip, chips))

    def store(j, carry):
        cross, square = carry
        a, b = acc[j], acc[chips + j]
        mine[j] = a
        theirs[j, 0:width] = b.astype(BF16)
        cross = cross + fold(wave[j].astype(F32) * a) + fold(wave[chips + j].astype(F32) * b)
        square = square + fold(vec[j].astype(F32) * a) + fold(vec[chips + j].astype(F32) * b)
        return cross, square

    zero = jnp.zeros((1, width), F32)
    rows = list(each(chips, store, (zero, zero))) + [keep[2 + i : 3 + i] for i in range(3)]
    theirs[0, width : width + TAIL] = tail_of(rows)
    for i, row in enumerate(rows):
        sums[i : i + 1] = row
    copy.wait()


def chip_kernel(at, count, mine, got, sums, base, *sends):
    width = mine.shape[2]
    rows = rows_of(got[0, width : width + TAIL], count)
    rows = [sums[at + i : at + i + 1] + rows[i] for i in range(count)]
    tail = tail_of(rows)

    def store(i, carry):
        base[i, 0:width] = mine[NEAR * i] + got[NEAR * i, 0:width].astype(F32)
        for k, send in enumerate(sends, 1):
            rel = NEAR * i + k
            send[i, 0:width] = (mine[rel] + got[rel, 0:width].astype(F32)).astype(BF16)
        return carry

    each(base.shape[0], store, 0)
    for send in sends:
        send[0, width : width + TAIL] = tail
    for i, row in enumerate(rows):
        base[0, width + i : width + i + 1] = row


def near_kernel(count, base, *refs):
    gots, out = refs[:-1], refs[-1]
    width = base.shape[2]
    parts = [[base[0, width + i : width + i + 1] for i in range(count)]]
    parts += [rows_of(got[0, width : width + TAIL], count) for got in gots]
    rows = [halve(jnp.concatenate([part[i] for part in parts], axis=0)) for i in range(count)]

    def store(i, carry):
        block = base[i, 0:width]
        for got in gots:
            block = block + got[i, 0:width].astype(F32)
        out[i, 0:width] = block
        for n, row in enumerate(rows):
            out[i, width + n : width + n + 1] = row
        return carry

    each(base.shape[0], store, 0)


def both_kernel(count, part, out):
    width = part.shape[2]
    block = part[1, 0:width]
    high = block.astype(BF16)
    out[0, 0:width] = high
    out[0, width : 2 * width] = (block - high.astype(F32)).astype(BF16)
    out[0, 2 * width : 3 * width] = part[0, 0:width].astype(BF16)
    out[0, 3 * width : 3 * width + TAIL] = tail_of(
        [part[0, width + i : width + i + 1] for i in range(count)]
    )


def far_kernel(count, part, out):
    width = part.shape[2]
    out[0, 0:width] = part[1, 0:width].astype(BF16)
    out[0, width : width + TAIL] = tail_of(
        [part[0, width + i : width + i + 1] for i in range(count)]
    )


def residual_kernel(part, got, wave, inside, precond, far, sums, sigma, resid, send, keep):
    width = part.shape[2]
    (ray,) = rows_of(got[0, 3 * width : 3 * width + TAIL], 1)
    norm, ray = total(sums[0:1]), total(part[0, width : width + 1] + ray)
    energy = ray / norm

    def piece(i):
        return got[0, i * width : (i + 1) * width].astype(F32)

    own = wave[0].astype(F32)
    first = (part[0, 0:width] + (piece(0) + piece(1))) * inside[0]
    q = precond[0] * (first - energy * own)
    low = q.astype(BF16)
    sigma[0] = first
    resid[0] = q
    send[0] = low
    there = (part[1, 0:width] + piece(2)) * inside[1]
    send[1] = (far[0] * (there - energy * wave[NEAR].astype(F32))).astype(BF16)
    rows = (norm, ray, fold(own * q), fold(low.astype(F32) * first), fold(q * q))
    for i, row in enumerate(rows):
        keep[i : i + 1] = row


def final_kernel(part, got, wave, inside, first, resid, keep, direction, sigma, subspace):
    width = part.shape[2]
    rows = rows_of(got[0, width : width + TAIL], 5)
    cross, square, inter, mixed, length = (
        total(part[0, width + i : width + i + 1] + rows[i]) for i in range(5)
    )
    norm, ray = keep[0:1], keep[1:2]
    c = inter / norm
    direction[0] = (resid[0] - c * wave[0].astype(F32)).astype(BF16)
    block = part[0, 0:width] + got[0, 0:width].astype(F32)
    sigma[0] = block * inside[0] - c * first[0]
    values = (
        ray,
        cross - c * ray,
        square - c * mixed - c * (cross - c * ray),
        length - 2.0 * c * inter + c * c * norm,
    )
    for i, value in enumerate(values):
        subspace[i] = jnp.max(value / norm)


VMEM = pl.BlockSpec(memory_space=pltpu.VMEM)
SMEM = pl.BlockSpec(memory_space=pltpu.SMEM)
HBM = pl.BlockSpec(memory_space=pl.ANY)


def call(kernel, name, ins, outs, scratch, args, flops, out_specs=None):
    moved = sum(a.size * a.dtype.itemsize for a in args)
    return pl.pallas_call(
        kernel,
        name=name,
        in_specs=ins,
        out_specs=out_specs or [VMEM] * len(outs),
        out_shape=outs,
        scratch_shapes=scratch,
        compiler_params=pltpu.CompilerParams(vmem_limit_bytes=LIMIT),
        cost_estimate=pl.CostEstimate(flops=flops, bytes_accessed=moved, transcendentals=0),
    )(*args)


def shape(*dims, dtype=F32):
    return jax.ShapeDtypeStruct(dims, dtype)


def swap(x):
    return lax.ppermute(x, "core", [(0, 1), (1, 0)])


def flip_chip(x, bits):
    chips = lax.axis_size("chip")
    return lax.ppermute(x, "chip", [(i, i ^ bits) for i in range(chips)])


def gather(block):
    step = NEAR * block.shape[0]
    while step < lax.axis_size("chip"):
        block = jnp.concatenate([block, flip_chip(block, step)], axis=0)
        step *= 2
    pieces = [block] + [flip_chip(block, k) for k in range(1, NEAR)]
    return pieces + [swap(piece) for piece in pieces]


def scatter(theirs, mine, sums, at, count):
    chips, width = mine.shape[0], mine.shape[2]
    span, high, wide = chips // NEAR, width + TAIL, width + 8
    sent = [shape(span, high, width, dtype=BF16)] * (NEAR - 1)
    base, *sends = call(
        lambda *refs: chip_kernel(at, count, *refs), "chip_sum", [VMEM] * 3,
        [shape(span, wide, width)] + sent, [], (mine, swap(theirs), sums), mine.size,
    )
    gots = [flip_chip(send, k) for k, send in enumerate(sends, 1)]
    (part,) = call(
        lambda *refs: near_kernel(count, *refs), "near_sum", [VMEM] * NEAR,
        [shape(span, wide, width)], [], (base, *gots), mine.size,
    )
    while span > 2:
        span //= 2
        part = part[:span] + flip_chip(part[span:], NEAR * span)
    return part


def shards(state, sector_sizes, left, right, source, target, precond):
    chips = lax.axis_size("chip")
    width = state.shape[1]
    high = width + TAIL
    every = 2 * chips
    flops = 4 * left.size * width
    near = [VMEM] * (2 * NEAR)
    block = shape(1, width, width)
    sums_of = shape(8, width)
    after_h = [shape(chips, high, width, dtype=BF16), shape(chips, width, width)]

    with jax.named_scope("own_mask"):
        (inside,) = call(
            mask_kernel, "own_mask", [SMEM], [shape(2, width, width)], [], (sector_sizes,), LONG
        )
    with jax.named_scope("gather_state"):
        pieces = gather(state)
        far = flip_chip(precond, NEAR)
    with jax.named_scope("first_sigma"):
        theirs, mine, wave, flip, sums = call(
            first_kernel, "first_sigma", [SMEM] * 3 + near + [VMEM] * 4,
            after_h + [shape(every, width, width, dtype=BF16), shape(*right.shape, dtype=BF16), sums_of],
            [pltpu.VMEM((every, width, width), F32), pltpu.VMEM((every, width), F32)],
            (source, target, sector_sizes, *pieces, left, right, inside, far), flops,
        )
    with jax.named_scope("sum_first"):
        part = scatter(theirs, mine, sums, 1, 1)
        (both,) = call(
            lambda *refs: both_kernel(1, *refs), "for_far", [VMEM],
            [shape(1, 3 * width + TAIL, width, dtype=BF16)], [], (part,), part.size,
        )
        got = flip_chip(both, NEAR)
    with jax.named_scope("residual"):
        first, resid, send, keep = call(
            residual_kernel, "residual", [VMEM] * 7,
            [block, block, shape(2, width, width, dtype=BF16), sums_of],
            [], (part, got, wave, inside, precond, far, sums), mine.size,
        )
    with jax.named_scope("gather_residual"):
        pieces = gather(send)
    with jax.named_scope("second_sigma"):
        theirs, mine, sums, sigma = call(
            second_kernel, "second_sigma", [SMEM] * 2 + near + [VMEM] * 5,
            after_h + [sums_of, block],
            [pltpu.VMEM((every, width, width), BF16), pltpu.VMEM((every, width, width), F32),
             pltpu.SemaphoreType.DMA],
            (source, target, *pieces, wave, left, flip, first, keep), flops,
            [VMEM] * 3 + [HBM],
        )
    with jax.named_scope("sum_second"):
        part = scatter(theirs, mine, sums, 0, 5)
        (both,) = call(
            lambda *refs: far_kernel(5, *refs), "for_far", [VMEM],
            [shape(1, high, width, dtype=BF16)], [], (part,), part.size,
        )
        got = flip_chip(both, NEAR)
    with jax.named_scope("outputs"):
        direction, second, subspace = call(
            final_kernel, "outputs", [VMEM] * 7,
            [shape(1, width, width, dtype=BF16), block, shape(4)],
            [], (part, got, wave, inside, first, resid, keep), mine.size, [VMEM, VMEM, SMEM],
        )
    return sigma, direction, second, subspace


def solution(mesh):
    groups, members = mesh.shape["grp"], mesh.shape["op"]
    split = Mesh(mesh.devices.reshape(groups, members // 2, 2), ("grp", "chip", "core"))
    rows = P(("grp", "chip", "core"))
    return jax.shard_map(
        shards,
        mesh=split,
        in_specs=(rows, P("grp"), rows, rows, rows, rows, rows),
        out_specs=(rows, rows, rows, P("grp")),
        check_vma=False,
    )
```

```python
import jax
import jax.numpy as jnp
from jax import lax
from jax.experimental import pallas as pl
from jax.experimental.pallas import tpu as pltpu
from jax.sharding import Mesh
from jax.sharding import PartitionSpec as P

BF16 = jnp.bfloat16
F32 = jnp.float32
TAIL = 16
LIMIT = 36 << 20
LONG = 10**11
NEAR = 4


def each(count, body, carry):
    if count <= 8:
        for j in range(count):
            carry = body(j, carry)
        return carry
    return lax.fori_loop(0, count, body, carry)


def mask_of(size, width):
    rows = lax.broadcasted_iota(jnp.int32, (width, width), 0)
    cols = lax.broadcasted_iota(jnp.int32, (width, width), 1)
    return (rows < size) & (cols < size)


def fold(x):
    return jnp.sum(x, axis=0, keepdims=True)


def eight(x):
    return jnp.sum(x.reshape(-1, 8, x.shape[1]), axis=0)


def at(i, width):
    if isinstance(i, int):
        return slice(i * width, (i + 1) * width)
    return pl.ds(pl.multiple_of(i * width, width), width)


def tail_of(rows):
    pieces = []
    for row in rows:
        rest = row
        for _ in range(3):
            piece = rest.astype(BF16).astype(F32)
            pieces.append(piece)
            rest = rest - piece
    lanes = rows[0].shape[1]
    place = lax.broadcasted_iota(jnp.int32, (TAIL, lanes), 0)
    tail = jnp.zeros((TAIL, lanes), F32)
    for at, piece in enumerate(pieces):
        tail = jnp.where(place == at, piece, tail)
    return tail.astype(BF16)


def rows_of(tail, count):
    wide = tail.astype(F32)
    return [
        (wide[3 * i : 3 * i + 1] + wide[3 * i + 1 : 3 * i + 2]) + wide[3 * i + 2 : 3 * i + 3]
        for i in range(count)
    ]


def total(row):
    return jnp.broadcast_to(jnp.sum(row, axis=1, keepdims=True), row.shape)


def halve(rows):
    while rows.shape[0] > 1:
        half = rows.shape[0] // 2
        rows = rows[:half] + rows[half:]
    return rows


def apply_blocks(plan, vec, left, right, acc, keep=None):
    terms, nnz = left.shape[0], left.shape[1]
    per = 6 if terms % 6 == 0 else 1

    def step(i, carry):
        items = [(i * per + k, n) for k in range(per) for n in range(nnz)]
        plans = [plan[k, n] for k, n in items]
        prods = [
            jnp.dot(left[k, n], vec[p & 1023], preferred_element_type=F32).astype(BF16)
            for (k, n), p in zip(items, plans)
        ]
        for (k, n), p, prod in zip(items, plans, prods):
            turned = right[k, n]
            if keep is not None:
                turned = turned.T
                keep[k, n] = turned
            acc[p >> 10] += jnp.dot(prod, turned, preferred_element_type=F32)
        return carry

    lax.fori_loop(0, terms // per, step, 0)


def mask_kernel(sizes, block, inside, limits, own):
    own[...] = block[...]
    chips, width = limits.shape[0] // 2, inside.shape[2]
    core, chip = lax.axis_index("core"), lax.axis_index("chip")
    for i in range(2):
        inside[i] = mask_of(sizes[2 * (chip ^ (NEAR * i)) + core], width).astype(F32)

    def size(j, carry):
        for other in range(2):
            row = jnp.full((1, width), sizes[2 * (chip ^ j) + (core ^ other)], jnp.int32)
            limits[pl.ds(other * chips + j, 1)] = row
        return carry

    each(chips, size, 0)


def plan_kernel(src, tgt, plan):
    chips = lax.axis_size("chip")
    chip, core = lax.axis_index("chip"), lax.axis_index("core")

    def place(s):
        return ((s >> 1) ^ chip) + chips * ((s ^ core) & 1)

    plan[...] = place(src[...]) | (place(tgt[...]) << 10)


def pair_kernel(own, far, out):
    out[0:1] = own[...]
    out[1:2] = far[...]


def first_kernel(*refs):
    pieces, ins, outs = refs[: 2 * NEAR], refs[2 * NEAR : 2 * NEAR + 5], refs[2 * NEAR + 5 :]
    plan, limits, left, right, _ = ins
    theirs, acc, wave, flip, sums, rows, places, sem = outs
    span, width = pieces[0].shape[0], pieces[0].shape[2]
    chips = NEAR * span
    copy = pltpu.make_async_copy(plan, places, sem)
    copy.start()
    across = lax.broadcasted_iota(jnp.int32, (width, width), 0)
    along = lax.broadcasted_iota(jnp.int32, (width, width), 1)
    acc[...] = jnp.zeros_like(acc)

    for other in range(2):
        for k in range(NEAR):
            piece = pieces[other * NEAR + k]

            def load(i, carry, other=other, k=k, piece=piece):
                rel = other * chips + NEAR * i + k
                limit = limits[pl.ds(rel, 1)]
                block = jnp.where((across < limit) & (along < limit), piece[i].astype(F32), 0.0)
                wave[rel] = block.astype(BF16)
                rows[rel] = eight(block * block)
                return carry

            each(span, load, 0)
    copy.wait()
    apply_blocks(places, wave, left, right, acc, flip)

    def store(j, ray):
        a, b = acc[j], acc[chips + j]
        theirs[at(j, width)] = b.astype(BF16)
        return ray + eight(wave[j].astype(F32) * a + wave[chips + j].astype(F32) * b)

    ray = fold(each(chips, store, jnp.zeros((8, width), F32)))
    theirs[chips * width :] = tail_of([ray])
    sums[0:1] = fold(halve(rows[...])[0])
    sums[1:2] = ray


def second_kernel(*refs):
    pieces, ins, outs = refs[: 2 * NEAR], refs[2 * NEAR : 2 * NEAR + 6], refs[2 * NEAR + 6 :]
    plan, wave, left, right, first, keep = ins
    theirs, acc, sums, sigma, vec, places, sems = outs
    span, width = pieces[0].shape[0], pieces[0].shape[2]
    chips = NEAR * span
    copy = pltpu.make_async_copy(plan, places, sems.at[0])
    result = pltpu.make_async_copy(first, sigma, sems.at[1])
    copy.start()
    result.start()
    acc[...] = jnp.zeros_like(acc)

    for other in range(2):
        for k in range(NEAR):
            piece = pieces[other * NEAR + k]

            def load(i, carry, other=other, k=k, piece=piece):
                vec[other * chips + NEAR * i + k] = piece[i]
                return carry

            each(span, load, 0)
    copy.wait()
    apply_blocks(places, vec, left, right, acc)

    def store(j, carry):
        cross, square = carry
        a, b = acc[j], acc[chips + j]
        theirs[at(j, width)] = b.astype(BF16)
        cross = cross + eight(wave[j].astype(F32) * a + wave[chips + j].astype(F32) * b)
        square = square + eight(vec[j].astype(F32) * a + vec[chips + j].astype(F32) * b)
        return cross, square

    zero = jnp.zeros((8, width), F32)
    rows = [fold(x) for x in each(chips, store, (zero, zero))]
    rows += [keep[2 + i : 3 + i] for i in range(3)]
    theirs[chips * width :] = tail_of(rows)
    for i, row in enumerate(rows):
        sums[i : i + 1] = row
    result.wait()


def chip_kernel(start, count, mine, got, sums, base, *sends):
    width = mine.shape[2]
    chips, span = mine.shape[0] // 2, base.shape[0]
    rows = rows_of(got[chips * width :], count)
    rows = [sums[start + i : start + i + 1] + rows[i] for i in range(count)]
    tail = tail_of(rows)

    def store(i, carry):
        base[i, 0:width] = mine[NEAR * i] + got[at(NEAR * i, width)].astype(F32)
        for k, send in enumerate(sends, 1):
            rel = NEAR * i + k
            send[at(i, width)] = (mine[rel] + got[at(rel, width)].astype(F32)).astype(BF16)
        return carry

    each(span, store, 0)
    for send in sends:
        send[span * width :] = tail
    for i, row in enumerate(rows):
        base[0, width + i : width + i + 1] = row


def near_kernel(count, base, *refs):
    gots, out = refs[:-1], refs[-1]
    span, width = base.shape[0], base.shape[2]
    parts = [[base[0, width + i : width + i + 1] for i in range(count)]]
    parts += [rows_of(got[span * width :], count) for got in gots]
    rows = [halve(jnp.concatenate([part[i] for part in parts], axis=0)) for i in range(count)]

    def store(i, carry):
        block = base[i, 0:width]
        for got in gots:
            block = block + got[at(i, width)].astype(F32)
        out[i, 0:width] = block
        for n, row in enumerate(rows):
            out[i, width + n : width + n + 1] = row
        return carry

    each(span, store, 0)


def both_kernel(count, part, out):
    width = part.shape[2]
    block = part[1, 0:width]
    high = block.astype(BF16)
    out[at(0, width)] = high
    out[at(1, width)] = (block - high.astype(F32)).astype(BF16)
    out[at(2, width)] = part[0, 0:width].astype(BF16)
    out[3 * width :] = tail_of([part[0, width + i : width + i + 1] for i in range(count)])


def far_kernel(count, part, out):
    width = part.shape[2]
    out[at(0, width)] = part[1, 0:width].astype(BF16)
    out[width:] = tail_of([part[0, width + i : width + i + 1] for i in range(count)])


def residual_kernel(part, got, wave, inside, precond, far, sums, sigma, resid, send, keep):
    width = part.shape[2]
    (ray,) = rows_of(got[3 * width :], 1)
    norm, ray = total(sums[0:1]), total(part[0, width : width + 1] + ray)
    energy = ray / norm

    def piece(i):
        return got[at(i, width)].astype(F32)

    own = wave[0].astype(F32)
    first = (part[0, 0:width] + (piece(0) + piece(1))) * inside[0]
    q = precond[0] * (first - energy * own)
    low = q.astype(BF16)
    sigma[0] = first
    resid[0] = q
    send[0] = low
    there = (part[1, 0:width] + piece(2)) * inside[1]
    send[1] = (far[0] * (there - energy * wave[NEAR].astype(F32))).astype(BF16)
    rows = (norm, ray, fold(own * q), fold(low.astype(F32) * first), fold(q * q))
    for i, row in enumerate(rows):
        keep[i : i + 1] = row


def final_kernel(part, got, wave, inside, first, resid, keep, direction, sigma, subspace):
    width = part.shape[2]
    rows = rows_of(got[width:], 5)
    cross, square, inter, mixed, length = (
        total(part[0, width + i : width + i + 1] + rows[i]) for i in range(5)
    )
    norm, ray = keep[0:1], keep[1:2]
    c = inter / norm
    direction[0] = (resid[0] - c * wave[0].astype(F32)).astype(BF16)
    block = part[0, 0:width] + got[at(0, width)].astype(F32)
    sigma[0] = block * inside[0] - c * first[0]
    values = (
        ray,
        cross - c * ray,
        square - c * mixed - c * (cross - c * ray),
        length - 2.0 * c * inter + c * c * norm,
    )
    for i, value in enumerate(values):
        subspace[i] = jnp.max(value / norm)


VMEM = pl.BlockSpec(memory_space=pltpu.VMEM)
SMEM = pl.BlockSpec(memory_space=pltpu.SMEM)
HBM = pl.BlockSpec(memory_space=pl.ANY)


def call(kernel, name, ins, outs, scratch, args, flops, out_specs=None):
    moved = sum(a.size * a.dtype.itemsize for a in args)
    return pl.pallas_call(
        kernel,
        name=name,
        in_specs=ins,
        out_specs=out_specs or [VMEM] * len(outs),
        out_shape=outs,
        scratch_shapes=scratch,
        compiler_params=pltpu.CompilerParams(vmem_limit_bytes=LIMIT),
        cost_estimate=pl.CostEstimate(flops=flops, bytes_accessed=moved, transcendentals=0),
    )(*args)


def shape(*dims, dtype=F32):
    return jax.ShapeDtypeStruct(dims, dtype)


def swap(x):
    return lax.ppermute(x, "core", [(0, 1), (1, 0)])


def flip_chip(x, bits):
    chips = lax.axis_size("chip")
    return lax.ppermute(x, "chip", [(i, i ^ bits) for i in range(chips)])


def gather(block):
    step = NEAR * block.shape[0]
    while step < lax.axis_size("chip"):
        block = jnp.concatenate([block, flip_chip(block, step)], axis=0)
        step *= 2
    pieces = [block] + [flip_chip(block, k) for k in range(1, NEAR)]
    return pieces + [swap(piece) for piece in pieces]


def scatter(theirs, mine, sums, start, count):
    chips, width = mine.shape[0] // 2, mine.shape[2]
    span, wide = chips // NEAR, width + 8
    sent = [shape(span * width + TAIL, width, dtype=BF16)] * (NEAR - 1)
    base, *sends = call(
        lambda *refs: chip_kernel(start, count, *refs), "chip_sum", [VMEM] * 3,
        [shape(span, wide, width)] + sent, [], (mine, swap(theirs), sums), mine.size,
    )
    gots = [flip_chip(send, k) for k, send in enumerate(sends, 1)]
    (part,) = call(
        lambda *refs: near_kernel(count, *refs), "near_sum", [VMEM] * NEAR,
        [shape(span, wide, width)], [], (base, *gots), mine.size,
    )
    while span > 2:
        span //= 2
        part = part[:span] + flip_chip(part[span:], NEAR * span)
    return part


def shards(state, sector_sizes, left, right, source, target, precond):
    chips = lax.axis_size("chip")
    width = state.shape[1]
    every = 2 * chips
    flops = 4 * left.size * width
    near = [VMEM] * (2 * NEAR)
    block = shape(1, width, width)
    sums_of = shape(8, width)
    after_h = [shape(chips * width + TAIL, width, dtype=BF16), shape(every, width, width)]
    vectors = shape(every, width, width, dtype=BF16)
    places = pltpu.SMEM(source.shape, jnp.int32)

    with jax.named_scope("plan"):
        (plan,) = call(
            plan_kernel, "plan", [VMEM] * 2, [shape(*source.shape, dtype=jnp.int32)], [],
            (source, target), source.size,
        )
        inside, limits, own = call(
            mask_kernel, "masks", [SMEM, VMEM],
            [shape(2, width, width), shape(every, width, dtype=jnp.int32),
             shape(1, width, width, dtype=BF16)],
            [], (sector_sizes, state), LONG,
        )
    with jax.named_scope("gather_state"):
        (pair,) = call(
            pair_kernel, "pair", [VMEM] * 2, [shape(2, width, width, dtype=BF16)], [],
            (own, flip_chip(state, NEAR)), state.size,
        )
        pieces = gather(pair)
        far = flip_chip(precond, NEAR)
    with jax.named_scope("first_sigma"):
        theirs, mine, wave, flip, sums = call(
            first_kernel, "first_sigma", near + [HBM] + [VMEM] * 4,
            after_h + [vectors, shape(*right.shape, dtype=BF16), sums_of],
            [pltpu.VMEM((every, 8, width), F32), places, pltpu.SemaphoreType.DMA],
            (*pieces, plan, limits, left, right, far), flops,
        )
    with jax.named_scope("sum_first"):
        part = scatter(theirs, mine, sums, 1, 1)
        (both,) = call(
            lambda *refs: both_kernel(1, *refs), "for_far", [VMEM],
            [shape(3 * width + TAIL, width, dtype=BF16)], [], (part,), part.size,
        )
        got = flip_chip(both, NEAR)
    with jax.named_scope("residual"):
        first, resid, send, keep = call(
            residual_kernel, "residual", [VMEM] * 7,
            [block, block, shape(2, width, width, dtype=BF16), sums_of],
            [], (part, got, wave, inside, precond, far, sums), mine.size,
        )
    with jax.named_scope("gather_residual"):
        pieces = gather(send)
    with jax.named_scope("second_sigma"):
        theirs, mine, sums, sigma = call(
            second_kernel, "second_sigma", near + [HBM] + [VMEM] * 5, after_h + [sums_of, block],
            [pltpu.VMEM((every, width, width), BF16), places, pltpu.SemaphoreType.DMA((2,))],
            (*pieces, plan, wave, left, flip, first, keep), flops, [VMEM] * 3 + [HBM],
        )
    with jax.named_scope("sum_second"):
        part = scatter(theirs, mine, sums, 0, 5)
        (both,) = call(
            lambda *refs: far_kernel(5, *refs), "for_far", [VMEM],
            [shape(width + TAIL, width, dtype=BF16)], [], (part,), part.size,
        )
        got = flip_chip(both, NEAR)
    with jax.named_scope("outputs"):
        direction, second, subspace = call(
            final_kernel, "outputs", [VMEM] * 7,
            [shape(1, width, width, dtype=BF16), block, shape(4)],
            [], (part, got, wave, inside, first, resid, keep), mine.size, [VMEM, VMEM, SMEM],
        )
    return sigma, direction, second, subspace


def solution(mesh):
    groups, members = mesh.shape["grp"], mesh.shape["op"]
    split = Mesh(mesh.devices.reshape(groups, members // 2, 2), ("grp", "chip", "core"))
    rows = P(("grp", "chip", "core"))
    return jax.shard_map(
        shards,
        mesh=split,
        in_specs=(rows, P("grp"), rows, rows, rows, rows, rows),
        out_specs=(rows, rows, rows, P("grp")),
        check_vma=False,
    )
```

```python
import functools

import jax
import jax.numpy as jnp
from jax import lax
from jax.experimental import pallas as pl
from jax.experimental.pallas import tpu as pltpu
from jax.sharding import Mesh
from jax.sharding import PartitionSpec as P

BF16 = jnp.bfloat16
F32 = jnp.float32
TAIL = 16
LIMIT = 36 << 20
LONG = 10**11
NEAR = 4


def each(count, body, carry):
    if count <= 8:
        for j in range(count):
            carry = body(j, carry)
        return carry
    return lax.fori_loop(0, count, body, carry)


def mask_of(size, width):
    rows = lax.broadcasted_iota(jnp.int32, (width, width), 0)
    cols = lax.broadcasted_iota(jnp.int32, (width, width), 1)
    return (rows < size) & (cols < size)


def fold(x):
    return jnp.sum(x, axis=0, keepdims=True)


def eight(x):
    return jnp.sum(x.reshape(-1, 8, x.shape[1]), axis=0)


def at(i, width):
    if isinstance(i, int):
        return slice(i * width, (i + 1) * width)
    return pl.ds(pl.multiple_of(i * width, width), width)


def tail_of(rows):
    pieces = []
    for row in rows:
        rest = row
        for _ in range(3):
            piece = rest.astype(BF16).astype(F32)
            pieces.append(piece)
            rest = rest - piece
    lanes = rows[0].shape[1]
    place = lax.broadcasted_iota(jnp.int32, (TAIL, lanes), 0)
    tail = jnp.zeros((TAIL, lanes), F32)
    for at, piece in enumerate(pieces):
        tail = jnp.where(place == at, piece, tail)
    return tail.astype(BF16)


def rows_of(tail, count):
    wide = tail.astype(F32)
    return [
        (wide[3 * i : 3 * i + 1] + wide[3 * i + 1 : 3 * i + 2]) + wide[3 * i + 2 : 3 * i + 3]
        for i in range(count)
    ]


def total(row):
    return jnp.broadcast_to(jnp.sum(row, axis=1, keepdims=True), row.shape)


def halve(rows):
    while rows.shape[0] > 1:
        half = rows.shape[0] // 2
        rows = rows[:half] + rows[half:]
    return rows


def apply_blocks(plan, vec, left, right, acc, keep=None):
    terms, nnz = left.shape[0], left.shape[1]
    per = 6 if terms % 6 == 0 else 1

    def step(i, carry):
        items = [(i * per + k, n) for k in range(per) for n in range(nnz)]
        plans = [plan[k, n] for k, n in items]
        prods = [
            jnp.dot(left[k, n], vec[p & 1023], preferred_element_type=F32).astype(BF16)
            for (k, n), p in zip(items, plans)
        ]
        for (k, n), p, prod in zip(items, plans, prods):
            turned = right[k, n]
            if keep is not None:
                turned = turned.T
                keep[k, n] = turned
            acc[p >> 10] += jnp.dot(prod, turned, preferred_element_type=F32)
        return carry

    lax.fori_loop(0, terms // per, step, 0)


def mask_kernel(sizes, block, inside, limits, own):
    own[...] = block[...]
    chips, width = limits.shape[0] // 2, inside.shape[2]
    core, chip = lax.axis_index("core"), lax.axis_index("chip")
    for i in range(2):
        inside[i] = mask_of(sizes[2 * (chip ^ (NEAR * i)) + core], width).astype(F32)

    def size(j, carry):
        for other in range(2):
            row = jnp.full((1, width), sizes[2 * (chip ^ j) + (core ^ other)], jnp.int32)
            limits[pl.ds(other * chips + j, 1)] = row
        return carry

    each(chips, size, 0)


def plan_kernel(src, tgt, plan):
    chips = lax.axis_size("chip")
    chip, core = lax.axis_index("chip"), lax.axis_index("core")

    def place(s):
        return ((s >> 1) ^ chip) + chips * ((s ^ core) & 1)

    plan[...] = place(src[...]) | (place(tgt[...]) << 10)


def pair_kernel(own, far, out):
    out[0:1] = own[...]
    out[1:2] = far[...]


def first_kernel(*refs):
    pieces, ins, outs = refs[: 2 * NEAR], refs[2 * NEAR : 2 * NEAR + 5], refs[2 * NEAR + 5 :]
    plan, limits, left, right, _ = ins
    theirs, (acc, wave, flip, sums, rows, places, sem) = outs[:NEAR], outs[NEAR:]
    span, width = pieces[0].shape[0], pieces[0].shape[2]
    chips = NEAR * span
    copy = pltpu.make_async_copy(plan, places, sem)
    copy.start()
    across = lax.broadcasted_iota(jnp.int32, (width, width), 0)
    along = lax.broadcasted_iota(jnp.int32, (width, width), 1)
    acc[...] = jnp.zeros_like(acc)

    for other in range(2):
        for k in range(NEAR):
            piece = pieces[other * NEAR + k]

            def load(i, carry, other=other, k=k, piece=piece):
                rel = other * chips + NEAR * i + k
                limit = limits[pl.ds(rel, 1)]
                block = jnp.where((across < limit) & (along < limit), piece[i].astype(F32), 0.0)
                wave[rel] = block.astype(BF16)
                rows[rel] = eight(block * block)
                return carry

            each(span, load, 0)
    copy.wait()
    apply_blocks(places, wave, left, right, acc, flip)

    def store(i, ray):
        for k in range(NEAR):
            j = NEAR * i + k
            a, b = acc[j], acc[chips + j]
            theirs[k][at(i, width)] = b.astype(BF16)
            ray = ray + eight(wave[j].astype(F32) * a + wave[chips + j].astype(F32) * b)
        return ray

    ray = fold(each(span, store, jnp.zeros((8, width), F32)))
    for part in theirs:
        part[span * width :] = tail_of([ray])
    sums[0:1] = fold(halve(rows[...])[0])
    sums[1:2] = ray


def second_kernel(*refs):
    pieces, ins, outs = refs[: 2 * NEAR], refs[2 * NEAR : 2 * NEAR + 6], refs[2 * NEAR + 6 :]
    plan, wave, left, right, first, keep = ins
    theirs, (acc, sums, sigma, vec, places, sems) = outs[:NEAR], outs[NEAR:]
    span, width = pieces[0].shape[0], pieces[0].shape[2]
    chips = NEAR * span
    copy = pltpu.make_async_copy(plan, places, sems.at[0])
    result = pltpu.make_async_copy(first, sigma, sems.at[1])
    copy.start()
    result.start()
    acc[...] = jnp.zeros_like(acc)

    for other in range(2):
        for k in range(NEAR):
            piece = pieces[other * NEAR + k]

            def load(i, carry, other=other, k=k, piece=piece):
                vec[other * chips + NEAR * i + k] = piece[i]
                return carry

            each(span, load, 0)
    copy.wait()
    apply_blocks(places, vec, left, right, acc)

    def store(i, carry):
        cross, square = carry
        for k in range(NEAR):
            j = NEAR * i + k
            a, b = acc[j], acc[chips + j]
            theirs[k][at(i, width)] = b.astype(BF16)
            cross = cross + eight(wave[j].astype(F32) * a + wave[chips + j].astype(F32) * b)
            square = square + eight(vec[j].astype(F32) * a + vec[chips + j].astype(F32) * b)
        return cross, square

    zero = jnp.zeros((8, width), F32)
    rows = [fold(x) for x in each(span, store, (zero, zero))]
    rows += [keep[2 + i : 3 + i] for i in range(3)]
    for part in theirs:
        part[span * width :] = tail_of(rows)
    for i, row in enumerate(rows):
        sums[i : i + 1] = row
    result.wait()


def chip_kernel(k, start, count, mine, got, sums, out):
    width = mine.shape[2]
    span = mine.shape[0] // 2 // NEAR
    rows = rows_of(got[span * width :], count)
    rows = [sums[start + i : start + i + 1] + rows[i] for i in range(count)]

    def store(i, carry):
        block = mine[NEAR * i + k] + got[at(i, width)].astype(F32)
        if k:
            out[at(i, width)] = block.astype(BF16)
        else:
            out[i, 0:width] = block
        return carry

    each(span, store, 0)
    if k:
        out[span * width :] = tail_of(rows)
    else:
        for i, row in enumerate(rows):
            out[0, width + i : width + i + 1] = row


def near_kernel(count, base, *refs):
    gots, out = refs[:-1], refs[-1]
    span, width = base.shape[0], base.shape[2]
    parts = [[base[0, width + i : width + i + 1] for i in range(count)]]
    parts += [rows_of(got[span * width :], count) for got in gots]
    rows = [halve(jnp.concatenate([part[i] for part in parts], axis=0)) for i in range(count)]

    def store(i, carry):
        block = base[i, 0:width]
        for got in gots:
            block = block + got[at(i, width)].astype(F32)
        out[i, 0:width] = block
        for n, row in enumerate(rows):
            out[i, width + n : width + n + 1] = row
        return carry

    each(span, store, 0)


def both_kernel(count, part, out):
    width = part.shape[2]
    block = part[1, 0:width]
    high = block.astype(BF16)
    out[at(0, width)] = high
    out[at(1, width)] = (block - high.astype(F32)).astype(BF16)
    out[at(2, width)] = part[0, 0:width].astype(BF16)
    out[3 * width :] = tail_of([part[0, width + i : width + i + 1] for i in range(count)])


def far_kernel(count, part, out):
    width = part.shape[2]
    out[at(0, width)] = part[1, 0:width].astype(BF16)
    out[width:] = tail_of([part[0, width + i : width + i + 1] for i in range(count)])


def residual_kernel(part, got, wave, inside, precond, far, sums, sigma, resid, send, keep):
    width = part.shape[2]
    (ray,) = rows_of(got[3 * width :], 1)
    norm, ray = total(sums[0:1]), total(part[0, width : width + 1] + ray)
    energy = ray / norm

    def piece(i):
        return got[at(i, width)].astype(F32)

    own = wave[0].astype(F32)
    first = (part[0, 0:width] + (piece(0) + piece(1))) * inside[0]
    q = precond[0] * (first - energy * own)
    low = q.astype(BF16)
    sigma[0] = first
    resid[0] = q
    send[0] = low
    there = (part[1, 0:width] + piece(2)) * inside[1]
    send[1] = (far[0] * (there - energy * wave[NEAR].astype(F32))).astype(BF16)
    rows = (norm, ray, fold(own * q), fold(low.astype(F32) * first), fold(q * q))
    for i, row in enumerate(rows):
        keep[i : i + 1] = row


def final_kernel(part, got, wave, inside, first, resid, keep, direction, sigma, subspace):
    width = part.shape[2]
    rows = rows_of(got[width:], 5)
    cross, square, inter, mixed, length = (
        total(part[0, width + i : width + i + 1] + rows[i]) for i in range(5)
    )
    norm, ray = keep[0:1], keep[1:2]
    c = inter / norm
    direction[0] = (resid[0] - c * wave[0].astype(F32)).astype(BF16)
    block = part[0, 0:width] + got[at(0, width)].astype(F32)
    sigma[0] = block * inside[0] - c * first[0]
    values = (
        ray,
        cross - c * ray,
        square - c * mixed - c * (cross - c * ray),
        length - 2.0 * c * inter + c * c * norm,
    )
    for i, value in enumerate(values):
        subspace[i] = jnp.max(value / norm)


VMEM = pl.BlockSpec(memory_space=pltpu.VMEM)
SMEM = pl.BlockSpec(memory_space=pltpu.SMEM)
HBM = pl.BlockSpec(memory_space=pl.ANY)


def call(kernel, name, ins, outs, scratch, args, flops, out_specs=None):
    moved = sum(a.size * a.dtype.itemsize for a in args)
    return pl.pallas_call(
        kernel,
        name=name,
        in_specs=ins,
        out_specs=out_specs or [VMEM] * len(outs),
        out_shape=outs,
        scratch_shapes=scratch,
        compiler_params=pltpu.CompilerParams(vmem_limit_bytes=LIMIT),
        cost_estimate=pl.CostEstimate(flops=flops, bytes_accessed=moved, transcendentals=0),
    )(*args)


def shape(*dims, dtype=F32):
    return jax.ShapeDtypeStruct(dims, dtype)


def swap(x):
    return lax.ppermute(x, "core", [(0, 1), (1, 0)])


def flip_chip(x, bits):
    chips = lax.axis_size("chip")
    return lax.ppermute(x, "chip", [(i, i ^ bits) for i in range(chips)])


def gather(block):
    step = NEAR * block.shape[0]
    while step < lax.axis_size("chip"):
        block = jnp.concatenate([block, flip_chip(block, step)], axis=0)
        step *= 2
    pieces = [block] + [flip_chip(block, k) for k in range(1, NEAR)]
    return pieces + [swap(piece) for piece in pieces]


def scatter(theirs, mine, sums, start, count):
    chips, width = mine.shape[0] // 2, mine.shape[2]
    span, wide = chips // NEAR, width + 8
    gots = [swap(part) for part in theirs[::-1]][::-1]
    sent = shape(span * width + TAIL, width, dtype=BF16)
    sends = [
        call(
            functools.partial(chip_kernel, k, start, count), "chip_sum", [VMEM] * 3,
            [sent if k else shape(span, wide, width)], [], (mine, gots[k], sums), mine.size // 4,
        )[0]
        for k in range(NEAR)
    ]
    base, *gots = [flip_chip(send, k) if k else send for k, send in enumerate(sends)]
    (part,) = call(
        lambda *refs: near_kernel(count, *refs), "near_sum", [VMEM] * NEAR,
        [shape(span, wide, width)], [], (base, *gots), mine.size,
    )
    while span > 2:
        span //= 2
        part = part[:span] + flip_chip(part[span:], NEAR * span)
    return part


def shards(state, sector_sizes, left, right, source, target, precond):
    chips = lax.axis_size("chip")
    width = state.shape[1]
    every = 2 * chips
    flops = 4 * left.size * width
    near = [VMEM] * (2 * NEAR)
    block = shape(1, width, width)
    sums_of = shape(8, width)
    theirs_of = shape(chips // NEAR * width + TAIL, width, dtype=BF16)
    after_h = [theirs_of] * NEAR + [shape(every, width, width)]
    vectors = shape(every, width, width, dtype=BF16)
    places = pltpu.SMEM(source.shape, jnp.int32)

    with jax.named_scope("plan"):
        (plan,) = call(
            plan_kernel, "plan", [VMEM] * 2, [shape(*source.shape, dtype=jnp.int32)], [],
            (source, target), source.size,
        )
        inside, limits, own = call(
            mask_kernel, "masks", [SMEM, VMEM],
            [shape(2, width, width), shape(every, width, dtype=jnp.int32),
             shape(1, width, width, dtype=BF16)],
            [], (sector_sizes, state), LONG,
        )
    with jax.named_scope("gather_state"):
        (pair,) = call(
            pair_kernel, "pair", [VMEM] * 2, [shape(2, width, width, dtype=BF16)], [],
            (own, flip_chip(state, NEAR)), state.size,
        )
        pieces = gather(pair)
        far = flip_chip(precond, NEAR)
    with jax.named_scope("first_sigma"):
        *theirs, mine, wave, flip, sums = call(
            first_kernel, "first_sigma", near + [HBM] + [VMEM] * 4,
            after_h + [vectors, shape(*right.shape, dtype=BF16), sums_of],
            [pltpu.VMEM((every, 8, width), F32), places, pltpu.SemaphoreType.DMA],
            (*pieces, plan, limits, left, right, far), flops,
        )
    with jax.named_scope("sum_first"):
        part = scatter(theirs, mine, sums, 1, 1)
        (both,) = call(
            lambda *refs: both_kernel(1, *refs), "for_far", [VMEM],
            [shape(3 * width + TAIL, width, dtype=BF16)], [], (part,), part.size,
        )
        got = flip_chip(both, NEAR)
    with jax.named_scope("residual"):
        first, resid, send, keep = call(
            residual_kernel, "residual", [VMEM] * 7,
            [block, block, shape(2, width, width, dtype=BF16), sums_of],
            [], (part, got, wave, inside, precond, far, sums), mine.size,
        )
    with jax.named_scope("gather_residual"):
        pieces = gather(send)
    with jax.named_scope("second_sigma"):
        *theirs, mine, sums, sigma = call(
            second_kernel, "second_sigma", near + [HBM] + [VMEM] * 5, after_h + [sums_of, block],
            [pltpu.VMEM((every, width, width), BF16), places, pltpu.SemaphoreType.DMA((2,))],
            (*pieces, plan, wave, left, flip, first, keep), flops, [VMEM] * (NEAR + 2) + [HBM],
        )
    with jax.named_scope("sum_second"):
        part = scatter(theirs, mine, sums, 0, 5)
        (both,) = call(
            lambda *refs: far_kernel(5, *refs), "for_far", [VMEM],
            [shape(width + TAIL, width, dtype=BF16)], [], (part,), part.size,
        )
        got = flip_chip(both, NEAR)
    with jax.named_scope("outputs"):
        direction, second, subspace = call(
            final_kernel, "outputs", [VMEM] * 7,
            [shape(1, width, width, dtype=BF16), block, shape(4)],
            [], (part, got, wave, inside, first, resid, keep), mine.size, [VMEM, VMEM, SMEM],
        )
    return sigma, direction, second, subspace


def solution(mesh):
    groups, members = mesh.shape["grp"], mesh.shape["op"]
    split = Mesh(mesh.devices.reshape(groups, members // 2, 2), ("grp", "chip", "core"))
    rows = P(("grp", "chip", "core"))
    return jax.shard_map(
        shards,
        mesh=split,
        in_specs=(rows, P("grp"), rows, rows, rows, rows, rows),
        out_specs=(rows, rows, rows, P("grp")),
        check_vma=False,
    )
```

```python
import jax
import jax.numpy as jnp
from jax import lax
from jax.experimental import pallas as pl
from jax.experimental.pallas import tpu as pltpu
from jax.sharding import Mesh
from jax.sharding import PartitionSpec as P

BF16 = jnp.bfloat16
F32 = jnp.float32
TAIL = 16
LIMIT = 36 << 20
LONG = 10**11
TINY = 1e-30
NEAR = 4


def each(count, body, carry):
    if count <= 8:
        for j in range(count):
            carry = body(j, carry)
        return carry
    return lax.fori_loop(0, count, body, carry)


def mask_of(size, width):
    rows = lax.broadcasted_iota(jnp.int32, (width, width), 0)
    cols = lax.broadcasted_iota(jnp.int32, (width, width), 1)
    return (rows < size) & (cols < size)


def fold(x):
    return jnp.sum(x, axis=0, keepdims=True)


def eight(x):
    return jnp.sum(x.reshape(-1, 8, x.shape[1]), axis=0)


def at(i, width):
    if isinstance(i, int):
        return slice(i * width, (i + 1) * width)
    return pl.ds(pl.multiple_of(i * width, width), width)


def tail_of(rows):
    pieces = []
    for row in rows:
        rest = row
        for _ in range(3):
            piece = rest.astype(BF16).astype(F32)
            pieces.append(piece)
            rest = rest - piece
    lanes = rows[0].shape[1]
    place = lax.broadcasted_iota(jnp.int32, (TAIL, lanes), 0)
    tail = jnp.zeros((TAIL, lanes), F32)
    for at, piece in enumerate(pieces):
        tail = jnp.where(place == at, piece, tail)
    return tail.astype(BF16)


def rows_of(tail, count):
    wide = tail.astype(F32)
    return [
        (wide[3 * i : 3 * i + 1] + wide[3 * i + 1 : 3 * i + 2]) + wide[3 * i + 2 : 3 * i + 3]
        for i in range(count)
    ]


def total(row):
    return jnp.broadcast_to(jnp.sum(row, axis=1, keepdims=True), row.shape)


def halve(rows):
    while rows.shape[0] > 1:
        half = rows.shape[0] // 2
        rows = rows[:half] + rows[half:]
    return rows


def apply_blocks(plan, vec, left, right, acc, keep=None):
    terms, nnz = left.shape[0], left.shape[1]
    per = 6 if terms % 6 == 0 else 1

    def step(i, carry):
        items = [(i * per + k, n) for k in range(per) for n in range(nnz)]
        plans = [plan[k, n] for k, n in items]
        prods = [
            jnp.dot(left[k, n], vec[p & 1023], preferred_element_type=F32).astype(BF16)
            for (k, n), p in zip(items, plans)
        ]
        for (k, n), p, prod in zip(items, plans, prods):
            turned = right[k, n]
            if keep is not None:
                turned = turned.T
                keep[k, n] = turned
            acc[p >> 10] += jnp.dot(prod, turned, preferred_element_type=F32)
        return carry

    lax.fori_loop(0, terms // per, step, 0)


def mask_kernel(sizes, block, inside, limits, own):
    own[...] = block[...]
    chips, width = limits.shape[0] // 2, inside.shape[2]
    core, chip = lax.axis_index("core"), lax.axis_index("chip")
    for i in range(2):
        inside[i] = mask_of(sizes[2 * (chip ^ (NEAR * i)) + core], width).astype(F32)

    def size(j, carry):
        for other in range(2):
            row = jnp.full((1, width), sizes[2 * (chip ^ j) + (core ^ other)], jnp.int32)
            limits[pl.ds(other * chips + j, 1)] = row
        return carry

    each(chips, size, 0)


def plan_kernel(src, tgt, plan):
    chips = lax.axis_size("chip")
    chip, core = lax.axis_index("chip"), lax.axis_index("core")

    def place(s):
        return ((s >> 1) ^ chip) + chips * ((s ^ core) & 1)

    plan[...] = place(src[...]) | (place(tgt[...]) << 10)


def pair_kernel(own, far, out):
    out[0:1] = own[...]
    out[1:2] = far[...]


def first_kernel(*refs):
    pieces, ins, outs = refs[: 2 * NEAR], refs[2 * NEAR : 2 * NEAR + 5], refs[2 * NEAR + 5 :]
    plan, limits, left, right, _ = ins
    theirs, acc, wave, flip, sums, rows, places, sem = outs
    span, width = pieces[0].shape[0], pieces[0].shape[2]
    chips = NEAR * span
    copy = pltpu.make_async_copy(plan, places, sem)
    copy.start()
    across = lax.broadcasted_iota(jnp.int32, (width, width), 0)
    along = lax.broadcasted_iota(jnp.int32, (width, width), 1)
    acc[...] = jnp.zeros_like(acc)

    for other in range(2):
        for k in range(NEAR):
            piece = pieces[other * NEAR + k]

            def load(i, carry, other=other, k=k, piece=piece):
                rel = other * chips + NEAR * i + k
                limit = limits[pl.ds(rel, 1)]
                block = jnp.where((across < limit) & (along < limit), piece[i].astype(F32), 0.0)
                wave[rel] = block.astype(BF16)
                rows[rel] = eight(block * block)
                return carry

            each(span, load, 0)
    copy.wait()
    apply_blocks(places, wave, left, right, acc, flip)

    def store(j, ray):
        a, b = acc[j], acc[chips + j]
        theirs[at(j, width)] = b.astype(BF16)
        return ray + eight(wave[j].astype(F32) * a + wave[chips + j].astype(F32) * b)

    ray = fold(each(chips, store, jnp.zeros((8, width), F32)))
    theirs[chips * width :] = tail_of([ray])
    sums[0:1] = ray


def second_kernel(*refs):
    pieces, ins, outs = refs[: 2 * NEAR], refs[2 * NEAR : 2 * NEAR + 6], refs[2 * NEAR + 6 :]
    plan, wave, left, right, first, keep = ins
    theirs, acc, sums, sigma, vec, places, sems = outs
    span, width = pieces[0].shape[0], pieces[0].shape[2]
    chips = NEAR * span
    copy = pltpu.make_async_copy(plan, places, sems.at[0])
    result = pltpu.make_async_copy(first, sigma, sems.at[1])
    copy.start()
    result.start()
    acc[...] = jnp.zeros_like(acc)

    for other in range(2):
        for k in range(NEAR):
            piece = pieces[other * NEAR + k]

            def load(i, carry, other=other, k=k, piece=piece):
                vec[other * chips + NEAR * i + k] = piece[i]
                return carry

            each(span, load, 0)
    copy.wait()
    apply_blocks(places, vec, left, right, acc)

    def store(j, carry):
        cross, square = carry
        a, b = acc[j], acc[chips + j]
        theirs[at(j, width)] = b.astype(BF16)
        cross = cross + eight(wave[j].astype(F32) * a + wave[chips + j].astype(F32) * b)
        square = square + eight(vec[j].astype(F32) * a + vec[chips + j].astype(F32) * b)
        return cross, square

    zero = jnp.zeros((8, width), F32)
    rows = [fold(x) for x in each(chips, store, (zero, zero))]
    rows += [keep[2 + i : 3 + i] for i in range(3)]
    theirs[chips * width :] = tail_of(rows)
    for i, row in enumerate(rows):
        sums[i : i + 1] = row
    result.wait()


def chip_kernel(start, count, mine, got, sums, base, *sends):
    width = mine.shape[2]
    chips, span = mine.shape[0] // 2, base.shape[0]
    rows = rows_of(got[chips * width :], count)
    rows = [sums[start + i : start + i + 1] + rows[i] for i in range(count)]
    tail = tail_of(rows)

    def store(i, carry):
        base[i, 0:width] = mine[NEAR * i] + got[at(NEAR * i, width)].astype(F32)
        for k, send in enumerate(sends, 1):
            rel = NEAR * i + k
            send[at(i, width)] = (mine[rel] + got[at(rel, width)].astype(F32)).astype(BF16)
        return carry

    each(span, store, 0)
    for send in sends:
        send[span * width :] = tail
    for i, row in enumerate(rows):
        base[0, width + i : width + i + 1] = row


def near_kernel(count, base, *refs):
    gots, out = refs[:-1], refs[-1]
    span, width = base.shape[0], base.shape[2]
    parts = [[base[0, width + i : width + i + 1] for i in range(count)]]
    parts += [rows_of(got[span * width :], count) for got in gots]
    rows = [halve(jnp.concatenate([part[i] for part in parts], axis=0)) for i in range(count)]

    def store(i, carry):
        block = base[i, 0:width]
        for got in gots:
            block = block + got[at(i, width)].astype(F32)
        out[i, 0:width] = block
        for n, row in enumerate(rows):
            out[i, width + n : width + n + 1] = row
        return carry

    each(span, store, 0)


def norm_kernel(rows, norms):
    norms[0:1] = total(fold(halve(rows[...])[0]))
    for i in range(2):
        norms[1 + i : 2 + i] = 1.0 / jnp.maximum(total(fold(rows[NEAR * i])), TINY)


def both_kernel(part, wave, norms, out):
    width = part.shape[2]
    rows = [part[0, width : width + 1]]
    for i in range(2):
        own = wave[NEAR * (1 - i)].astype(F32)
        block = part[1 - i, 0:width]
        share = total(fold(block * own)) * norms[2 - i : 3 - i]
        out[at(i, width)] = (block - share * own).astype(BF16)
        rows.append(share)
    out[2 * width :] = tail_of(rows)


def far_kernel(count, part, out):
    width = part.shape[2]
    out[at(0, width)] = part[1, 0:width].astype(BF16)
    out[width:] = tail_of([part[0, width + i : width + i + 1] for i in range(count)])


def residual_kernel(part, got, wave, inside, precond, far, norms, sigma, resid, send, keep):
    width = part.shape[2]
    ray, *shares = rows_of(got[2 * width :], 3)
    norm, ray = norms[0:1], total(part[0, width : width + 1] + ray)
    energy = ray / norm
    own, other = wave[0].astype(F32), wave[NEAR].astype(F32)
    first = part[0, 0:width] + (got[at(0, width)].astype(F32) + shares[0] * own)
    first = first * inside[0]
    q = precond[0] * (first - energy * own)
    low = q.astype(BF16)
    sigma[0] = first
    resid[0] = q
    send[0] = low
    there = part[1, 0:width] + (got[at(1, width)].astype(F32) + shares[1] * other)
    send[1] = (far[0] * (there * inside[1] - energy * other)).astype(BF16)
    rows = (norm, ray, fold(own * q), fold(low.astype(F32) * first), fold(q * q))
    for i, row in enumerate(rows):
        keep[i : i + 1] = row


def final_kernel(part, got, wave, inside, first, resid, keep, direction, sigma, subspace):
    width = part.shape[2]
    rows = rows_of(got[width:], 5)
    cross, square, inter, mixed, length = (
        total(part[0, width + i : width + i + 1] + rows[i]) for i in range(5)
    )
    norm, ray = keep[0:1], keep[1:2]
    c = inter / norm
    direction[0] = (resid[0] - c * wave[0].astype(F32)).astype(BF16)
    block = part[0, 0:width] + got[at(0, width)].astype(F32)
    sigma[0] = block * inside[0] - c * first[0]
    values = (
        ray,
        cross - c * ray,
        square - c * mixed - c * (cross - c * ray),
        length - 2.0 * c * inter + c * c * norm,
    )
    for i, value in enumerate(values):
        subspace[i] = jnp.max(value / norm)


VMEM = pl.BlockSpec(memory_space=pltpu.VMEM)
SMEM = pl.BlockSpec(memory_space=pltpu.SMEM)
HBM = pl.BlockSpec(memory_space=pl.ANY)


def call(kernel, name, ins, outs, scratch, args, flops, out_specs=None):
    moved = sum(a.size * a.dtype.itemsize for a in args)
    return pl.pallas_call(
        kernel,
        name=name,
        in_specs=ins,
        out_specs=out_specs or [VMEM] * len(outs),
        out_shape=outs,
        scratch_shapes=scratch,
        compiler_params=pltpu.CompilerParams(vmem_limit_bytes=LIMIT),
        cost_estimate=pl.CostEstimate(flops=flops, bytes_accessed=moved, transcendentals=0),
    )(*args)


def shape(*dims, dtype=F32):
    return jax.ShapeDtypeStruct(dims, dtype)


def swap(x):
    return lax.ppermute(x, "core", [(0, 1), (1, 0)])


def flip_chip(x, bits):
    chips = lax.axis_size("chip")
    return lax.ppermute(x, "chip", [(i, i ^ bits) for i in range(chips)])


def gather(block):
    step = NEAR * block.shape[0]
    while step < lax.axis_size("chip"):
        block = jnp.concatenate([block, flip_chip(block, step)], axis=0)
        step *= 2
    pieces = [block] + [flip_chip(block, k) for k in range(1, NEAR)]
    return pieces + [swap(piece) for piece in pieces]


def scatter(theirs, mine, sums, start, count):
    chips, width = mine.shape[0] // 2, mine.shape[2]
    span, wide = chips // NEAR, width + 8
    sent = [shape(span * width + TAIL, width, dtype=BF16)] * (NEAR - 1)
    base, *sends = call(
        lambda *refs: chip_kernel(start, count, *refs), "chip_sum", [VMEM] * 3,
        [shape(span, wide, width)] + sent, [], (mine, swap(theirs), sums), mine.size,
    )
    gots = [flip_chip(send, k) for k, send in enumerate(sends, 1)]
    (part,) = call(
        lambda *refs: near_kernel(count, *refs), "near_sum", [VMEM] * NEAR,
        [shape(span, wide, width)], [], (base, *gots), mine.size,
    )
    while span > 2:
        span //= 2
        part = part[:span] + flip_chip(part[span:], NEAR * span)
    return part


def shards(state, sector_sizes, left, right, source, target, precond):
    chips = lax.axis_size("chip")
    width = state.shape[1]
    every = 2 * chips
    flops = 4 * left.size * width
    near = [VMEM] * (2 * NEAR)
    block = shape(1, width, width)
    sums_of = shape(8, width)
    after_h = [shape(chips * width + TAIL, width, dtype=BF16), shape(every, width, width)]
    vectors = shape(every, width, width, dtype=BF16)
    places = pltpu.SMEM(source.shape, jnp.int32)

    with jax.named_scope("plan"):
        (plan,) = call(
            plan_kernel, "plan", [VMEM] * 2, [shape(*source.shape, dtype=jnp.int32)], [],
            (source, target), source.size,
        )
        inside, limits, own = call(
            mask_kernel, "masks", [SMEM, VMEM],
            [shape(2, width, width), shape(every, width, dtype=jnp.int32),
             shape(1, width, width, dtype=BF16)],
            [], (sector_sizes, state), LONG,
        )
    with jax.named_scope("gather_state"):
        (pair,) = call(
            pair_kernel, "pair", [VMEM] * 2, [shape(2, width, width, dtype=BF16)], [],
            (own, flip_chip(state, NEAR)), state.size,
        )
        pieces = gather(pair)
        far = flip_chip(precond, NEAR)
    with jax.named_scope("first_sigma"):
        theirs, mine, wave, flip, sums, rows = call(
            first_kernel, "first_sigma", near + [HBM] + [VMEM] * 4,
            after_h + [vectors, shape(*right.shape, dtype=BF16), sums_of, shape(every, 8, width)],
            [places, pltpu.SemaphoreType.DMA],
            (*pieces, plan, limits, left, right, far), flops,
        )
    with jax.named_scope("sum_first"):
        (norms,) = call(norm_kernel, "norms", [VMEM], [sums_of], [], (rows,), rows.size)
        part = scatter(theirs, mine, sums, 0, 1)
        (both,) = call(
            both_kernel, "for_far", [VMEM] * 3, [shape(2 * width + TAIL, width, dtype=BF16)], [],
            (part, wave, norms), part.size,
        )
        got = flip_chip(both, NEAR)
    with jax.named_scope("residual"):
        first, resid, send, keep = call(
            residual_kernel, "residual", [VMEM] * 7,
            [block, block, shape(2, width, width, dtype=BF16), sums_of],
            [], (part, got, wave, inside, precond, far, norms), mine.size,
        )
    with jax.named_scope("gather_residual"):
        pieces = gather(send)
    with jax.named_scope("second_sigma"):
        theirs, mine, sums, sigma = call(
            second_kernel, "second_sigma", near + [HBM] + [VMEM] * 5, after_h + [sums_of, block],
            [pltpu.VMEM((every, width, width), BF16), places, pltpu.SemaphoreType.DMA((2,))],
            (*pieces, plan, wave, left, flip, first, keep), flops, [VMEM] * 3 + [HBM],
        )
    with jax.named_scope("sum_second"):
        part = scatter(theirs, mine, sums, 0, 5)
        (both,) = call(
            lambda *refs: far_kernel(5, *refs), "for_far", [VMEM],
            [shape(width + TAIL, width, dtype=BF16)], [], (part,), part.size,
        )
        got = flip_chip(both, NEAR)
    with jax.named_scope("outputs"):
        direction, second, subspace = call(
            final_kernel, "outputs", [VMEM] * 7,
            [shape(1, width, width, dtype=BF16), block, shape(4)],
            [], (part, got, wave, inside, first, resid, keep), mine.size, [VMEM, VMEM, SMEM],
        )
    return sigma, direction, second, subspace


def solution(mesh):
    groups, members = mesh.shape["grp"], mesh.shape["op"]
    split = Mesh(mesh.devices.reshape(groups, members // 2, 2), ("grp", "chip", "core"))
    rows = P(("grp", "chip", "core"))
    return jax.shard_map(
        shards,
        mesh=split,
        in_specs=(rows, P("grp"), rows, rows, rows, rows, rows),
        out_specs=(rows, rows, rows, P("grp")),
        check_vma=False,
    )
```

```python
import jax
import jax.numpy as jnp
from jax import lax
from jax.experimental import pallas as pl
from jax.experimental.pallas import tpu as pltpu
from jax.sharding import Mesh
from jax.sharding import PartitionSpec as P

BF16 = jnp.bfloat16
F32 = jnp.float32
TAIL = 16
LIMIT = 36 << 20
LONG = 10**11
TINY = 1e-30
NEAR = 4
GATHER = ((1, 2, 3), (1, 2, 3))
SUMS = ((3, 1, 2), (2, 1, 3))


def each(count, body, carry):
    if count <= 8:
        for j in range(count):
            carry = body(j, carry)
        return carry
    return lax.fori_loop(0, count, body, carry)


def mask_of(size, width):
    rows = lax.broadcasted_iota(jnp.int32, (width, width), 0)
    cols = lax.broadcasted_iota(jnp.int32, (width, width), 1)
    return (rows < size) & (cols < size)


def fold(x):
    return jnp.sum(x, axis=0, keepdims=True)


def eight(x):
    return jnp.sum(x.reshape(-1, 8, x.shape[1]), axis=0)


def at(i, width):
    if isinstance(i, int):
        return slice(i * width, (i + 1) * width)
    return pl.ds(pl.multiple_of(i * width, width), width)


def tail_of(rows):
    pieces = []
    for row in rows:
        rest = row
        for _ in range(3):
            piece = rest.astype(BF16).astype(F32)
            pieces.append(piece)
            rest = rest - piece
    lanes = rows[0].shape[1]
    place = lax.broadcasted_iota(jnp.int32, (TAIL, lanes), 0)
    tail = jnp.zeros((TAIL, lanes), F32)
    for at, piece in enumerate(pieces):
        tail = jnp.where(place == at, piece, tail)
    return tail.astype(BF16)


def rows_of(tail, count):
    wide = tail.astype(F32)
    return [
        (wide[3 * i : 3 * i + 1] + wide[3 * i + 1 : 3 * i + 2]) + wide[3 * i + 2 : 3 * i + 3]
        for i in range(count)
    ]


def total(row):
    return jnp.broadcast_to(jnp.sum(row, axis=1, keepdims=True), row.shape)


def halve(rows):
    while rows.shape[0] > 1:
        half = rows.shape[0] // 2
        rows = rows[:half] + rows[half:]
    return rows


def near_of(orders, core, n):
    if n == 0:
        return 0
    first, second = (order[n - 1] for order in orders)
    return first + (second - first) * core


def apply_blocks(plan, vec, left, right, acc, keep=None):
    terms, nnz = left.shape[0], left.shape[1]
    per = 6 if terms % 6 == 0 else 1

    def step(i, carry):
        items = [(i * per + k, n) for k in range(per) for n in range(nnz)]
        plans = [plan[k, n] for k, n in items]
        prods = [
            jnp.dot(left[k, n], vec[p & 1023], preferred_element_type=F32).astype(BF16)
            for (k, n), p in zip(items, plans)
        ]
        for (k, n), p, prod in zip(items, plans, prods):
            turned = right[k, n]
            if keep is not None:
                turned = turned.T
                keep[k, n] = turned
            acc[p >> 10] += jnp.dot(prod, turned, preferred_element_type=F32)
        return carry

    lax.fori_loop(0, terms // per, step, 0)


def mask_kernel(sizes, block, inside, limits, own):
    own[...] = block[...]
    chips, width = limits.shape[0] // 2, inside.shape[2]
    core, chip = lax.axis_index("core"), lax.axis_index("chip")
    for i in range(2):
        inside[i] = mask_of(sizes[2 * (chip ^ (NEAR * i)) + core], width).astype(F32)

    def size(j, carry):
        for other in range(2):
            row = jnp.full((1, width), sizes[2 * (chip ^ j) + (core ^ other)], jnp.int32)
            limits[pl.ds(other * chips + j, 1)] = row
        return carry

    each(chips, size, 0)


def plan_kernel(src, tgt, plan):
    chips = lax.axis_size("chip")
    chip, core = lax.axis_index("chip"), lax.axis_index("core")

    def place(s):
        return ((s >> 1) ^ chip) + chips * ((s ^ core) & 1)

    plan[...] = place(src[...]) | (place(tgt[...]) << 10)


def pair_kernel(own, far, out):
    out[0:1] = own[...]
    out[1:2] = far[...]


def first_kernel(*refs):
    pieces, ins, outs = refs[: 2 * NEAR], refs[2 * NEAR : 2 * NEAR + 5], refs[2 * NEAR + 5 :]
    plan, limits, left, right, _ = ins
    theirs, acc, wave, flip, sums, rows, places, sem = outs
    span, width = pieces[0].shape[0], pieces[0].shape[2]
    chips = NEAR * span
    core = lax.axis_index("core")
    copy = pltpu.make_async_copy(plan, places, sem)
    copy.start()
    across = lax.broadcasted_iota(jnp.int32, (width, width), 0)
    along = lax.broadcasted_iota(jnp.int32, (width, width), 1)
    acc[...] = jnp.zeros_like(acc)

    for other in range(2):
        for k in range(NEAR):
            piece = pieces[other * NEAR + k]

            def load(i, carry, other=other, k=k, piece=piece):
                rel = other * chips + NEAR * i + near_of(GATHER, core ^ other, k)
                limit = limits[pl.ds(rel, 1)]
                block = jnp.where((across < limit) & (along < limit), piece[i].astype(F32), 0.0)
                wave[rel] = block.astype(BF16)
                rows[rel] = eight(block * block)
                return carry

            each(span, load, 0)
    copy.wait()
    apply_blocks(places, wave, left, right, acc, flip)

    def store(j, ray):
        a, b = acc[j], acc[chips + j]
        theirs[at(j, width)] = b.astype(BF16)
        return ray + eight(wave[j].astype(F32) * a + wave[chips + j].astype(F32) * b)

    ray = fold(each(chips, store, jnp.zeros((8, width), F32)))
    theirs[chips * width :] = tail_of([ray])
    sums[0:1] = ray


def second_kernel(*refs):
    pieces, ins, outs = refs[: 2 * NEAR], refs[2 * NEAR : 2 * NEAR + 6], refs[2 * NEAR + 6 :]
    plan, wave, left, right, first, keep = ins
    theirs, acc, sums, sigma, vec, places, sems = outs
    span, width = pieces[0].shape[0], pieces[0].shape[2]
    chips = NEAR * span
    core = lax.axis_index("core")
    copy = pltpu.make_async_copy(plan, places, sems.at[0])
    result = pltpu.make_async_copy(first, sigma, sems.at[1])
    copy.start()
    result.start()
    acc[...] = jnp.zeros_like(acc)

    for other in range(2):
        for k in range(NEAR):
            piece = pieces[other * NEAR + k]

            def load(i, carry, other=other, k=k, piece=piece):
                vec[other * chips + NEAR * i + near_of(GATHER, core ^ other, k)] = piece[i]
                return carry

            each(span, load, 0)
    copy.wait()
    apply_blocks(places, vec, left, right, acc)

    def store(j, carry):
        cross, square = carry
        a, b = acc[j], acc[chips + j]
        theirs[at(j, width)] = b.astype(BF16)
        cross = cross + eight(wave[j].astype(F32) * a + wave[chips + j].astype(F32) * b)
        square = square + eight(vec[j].astype(F32) * a + vec[chips + j].astype(F32) * b)
        return cross, square

    zero = jnp.zeros((8, width), F32)
    rows = [fold(x) for x in each(chips, store, (zero, zero))]
    rows += [keep[2 + i : 3 + i] for i in range(3)]
    theirs[chips * width :] = tail_of(rows)
    for i, row in enumerate(rows):
        sums[i : i + 1] = row
    result.wait()


def chip_kernel(start, count, mine, got, sums, base, *sends):
    width = mine.shape[2]
    chips, span = mine.shape[0] // 2, base.shape[0]
    core = lax.axis_index("core")
    rows = rows_of(got[chips * width :], count)
    rows = [sums[start + i : start + i + 1] + rows[i] for i in range(count)]
    tail = tail_of(rows)

    def store(i, carry):
        base[i, 0:width] = mine[NEAR * i] + got[at(NEAR * i, width)].astype(F32)
        for n, send in enumerate(sends, 1):
            rel = NEAR * i + near_of(SUMS, core, n)
            send[at(i, width)] = (mine[rel] + got[at(rel, width)].astype(F32)).astype(BF16)
        return carry

    each(span, store, 0)
    for send in sends:
        send[span * width :] = tail
    for i, row in enumerate(rows):
        base[0, width + i : width + i + 1] = row


def near_kernel(count, base, *refs):
    gots, out = refs[:-1], refs[-1]
    span, width = base.shape[0], base.shape[2]
    parts = [[base[0, width + i : width + i + 1] for i in range(count)]]
    came = [rows_of(got[span * width :], count) for got in gots]
    first = lax.axis_index("core") == 0
    for k in range(1, NEAR):
        a, b = (came[order.index(k)] for order in SUMS)
        parts.append([jnp.where(first, x, y) for x, y in zip(a, b)])
    rows = [halve(jnp.concatenate([part[i] for part in parts], axis=0)) for i in range(count)]

    def store(i, carry):
        block = base[i, 0:width]
        for got in gots:
            block = block + got[at(i, width)].astype(F32)
        out[i, 0:width] = block
        for n, row in enumerate(rows):
            out[i, width + n : width + n + 1] = row
        return carry

    each(span, store, 0)


def norm_kernel(rows, norms):
    norms[0:1] = total(fold(halve(rows[...])[0]))
    for i in range(2):
        norms[1 + i : 2 + i] = 1.0 / jnp.maximum(total(fold(rows[NEAR * i])), TINY)


def both_kernel(part, wave, norms, out):
    width = part.shape[2]
    rows = [part[0, width : width + 1]]
    for i in range(2):
        own = wave[NEAR * (1 - i)].astype(F32)
        block = part[1 - i, 0:width]
        share = total(fold(block * own)) * norms[2 - i : 3 - i]
        out[at(i, width)] = (block - share * own).astype(BF16)
        rows.append(share)
    out[2 * width :] = tail_of(rows)


def far_kernel(count, part, out):
    width = part.shape[2]
    out[at(0, width)] = part[1, 0:width].astype(BF16)
    out[width:] = tail_of([part[0, width + i : width + i + 1] for i in range(count)])


def residual_kernel(part, got, wave, inside, precond, far, norms, sigma, resid, send, keep):
    width = part.shape[2]
    ray, *shares = rows_of(got[2 * width :], 3)
    norm, ray = norms[0:1], total(part[0, width : width + 1] + ray)
    energy = ray / norm
    own, other = wave[0].astype(F32), wave[NEAR].astype(F32)
    first = part[0, 0:width] + (got[at(0, width)].astype(F32) + shares[0] * own)
    first = first * inside[0]
    q = precond[0] * (first - energy * own)
    low = q.astype(BF16)
    sigma[0] = first
    resid[0] = q
    send[0] = low
    there = part[1, 0:width] + (got[at(1, width)].astype(F32) + shares[1] * other)
    send[1] = (far[0] * (there * inside[1] - energy * other)).astype(BF16)
    rows = (norm, ray, fold(own * q), fold(low.astype(F32) * first), fold(q * q))
    for i, row in enumerate(rows):
        keep[i : i + 1] = row


def final_kernel(part, got, wave, inside, first, resid, keep, direction, sigma, subspace):
    width = part.shape[2]
    rows = rows_of(got[width:], 5)
    cross, square, inter, mixed, length = (
        total(part[0, width + i : width + i + 1] + rows[i]) for i in range(5)
    )
    norm, ray = keep[0:1], keep[1:2]
    c = inter / norm
    direction[0] = (resid[0] - c * wave[0].astype(F32)).astype(BF16)
    block = part[0, 0:width] + got[at(0, width)].astype(F32)
    sigma[0] = block * inside[0] - c * first[0]
    values = (
        ray,
        cross - c * ray,
        square - c * mixed - c * (cross - c * ray),
        length - 2.0 * c * inter + c * c * norm,
    )
    for i, value in enumerate(values):
        subspace[i] = jnp.max(value / norm)


VMEM = pl.BlockSpec(memory_space=pltpu.VMEM)
SMEM = pl.BlockSpec(memory_space=pltpu.SMEM)
HBM = pl.BlockSpec(memory_space=pl.ANY)


def call(kernel, name, ins, outs, scratch, args, flops, out_specs=None):
    moved = sum(a.size * a.dtype.itemsize for a in args)
    return pl.pallas_call(
        kernel,
        name=name,
        in_specs=ins,
        out_specs=out_specs or [VMEM] * len(outs),
        out_shape=outs,
        scratch_shapes=scratch,
        compiler_params=pltpu.CompilerParams(vmem_limit_bytes=LIMIT),
        cost_estimate=pl.CostEstimate(flops=flops, bytes_accessed=moved, transcendentals=0),
    )(*args)


def shape(*dims, dtype=F32):
    return jax.ShapeDtypeStruct(dims, dtype)


def swap(x):
    return lax.ppermute(x, "core", [(0, 1), (1, 0)])


def flip_chip(x, bits):
    chips = lax.axis_size("chip")
    return lax.ppermute(x, "chip", [(i, i ^ bits) for i in range(chips)])


def flip_near(x, orders, n):
    chips = lax.axis_size("chip")
    pairs = [(2 * i + c, 2 * (i ^ near_of(orders, c, n)) + c) for i in range(chips) for c in range(2)]
    return lax.ppermute(x, ("chip", "core"), pairs)


def gather(block):
    step = NEAR * block.shape[0]
    while step < lax.axis_size("chip"):
        block = jnp.concatenate([block, flip_chip(block, step)], axis=0)
        step *= 2
    pieces = [block] + [flip_near(block, GATHER, n) for n in range(1, NEAR)]
    return pieces + [swap(piece) for piece in pieces]


def scatter(theirs, mine, sums, start, count):
    chips, width = mine.shape[0] // 2, mine.shape[2]
    span, wide = chips // NEAR, width + 8
    sent = [shape(span * width + TAIL, width, dtype=BF16)] * (NEAR - 1)
    base, *sends = call(
        lambda *refs: chip_kernel(start, count, *refs), "chip_sum", [VMEM] * 3,
        [shape(span, wide, width)] + sent, [], (mine, swap(theirs), sums), mine.size,
    )
    gots = [flip_near(send, SUMS, n) for n, send in enumerate(sends, 1)]
    (part,) = call(
        lambda *refs: near_kernel(count, *refs), "near_sum", [VMEM] * NEAR,
        [shape(span, wide, width)], [], (base, *gots), mine.size,
    )
    while span > 2:
        span //= 2
        part = part[:span] + flip_chip(part[span:], NEAR * span)
    return part


def shards(state, sector_sizes, left, right, source, target, precond):
    chips = lax.axis_size("chip")
    width = state.shape[1]
    every = 2 * chips
    flops = 4 * left.size * width
    near = [VMEM] * (2 * NEAR)
    block = shape(1, width, width)
    sums_of = shape(8, width)
    after_h = [shape(chips * width + TAIL, width, dtype=BF16), shape(every, width, width)]
    vectors = shape(every, width, width, dtype=BF16)
    places = pltpu.SMEM(source.shape, jnp.int32)

    with jax.named_scope("plan"):
        (plan,) = call(
            plan_kernel, "plan", [VMEM] * 2, [shape(*source.shape, dtype=jnp.int32)], [],
            (source, target), source.size,
        )
        inside, limits, own = call(
            mask_kernel, "masks", [SMEM, VMEM],
            [shape(2, width, width), shape(every, width, dtype=jnp.int32),
             shape(1, width, width, dtype=BF16)],
            [], (sector_sizes, state), LONG,
        )
    with jax.named_scope("gather_state"):
        (pair,) = call(
            pair_kernel, "pair", [VMEM] * 2, [shape(2, width, width, dtype=BF16)], [],
            (own, flip_chip(state, NEAR)), state.size,
        )
        pieces = gather(pair)
        far = flip_chip(precond, NEAR)
    with jax.named_scope("first_sigma"):
        theirs, mine, wave, flip, sums, rows = call(
            first_kernel, "first_sigma", near + [HBM] + [VMEM] * 4,
            after_h + [vectors, shape(*right.shape, dtype=BF16), sums_of, shape(every, 8, width)],
            [places, pltpu.SemaphoreType.DMA],
            (*pieces, plan, limits, left, right, far), flops,
        )
    with jax.named_scope("sum_first"):
        (norms,) = call(norm_kernel, "norms", [VMEM], [sums_of], [], (rows,), rows.size)
        part = scatter(theirs, mine, sums, 0, 1)
        (both,) = call(
            both_kernel, "for_far", [VMEM] * 3, [shape(2 * width + TAIL, width, dtype=BF16)], [],
            (part, wave, norms), part.size,
        )
        got = flip_chip(both, NEAR)
    with jax.named_scope("residual"):
        first, resid, send, keep = call(
            residual_kernel, "residual", [VMEM] * 7,
            [block, block, shape(2, width, width, dtype=BF16), sums_of],
            [], (part, got, wave, inside, precond, far, norms), mine.size,
        )
    with jax.named_scope("gather_residual"):
        pieces = gather(send)
    with jax.named_scope("second_sigma"):
        theirs, mine, sums, sigma = call(
            second_kernel, "second_sigma", near + [HBM] + [VMEM] * 5, after_h + [sums_of, block],
            [pltpu.VMEM((every, width, width), BF16), places, pltpu.SemaphoreType.DMA((2,))],
            (*pieces, plan, wave, left, flip, first, keep), flops, [VMEM] * 3 + [HBM],
        )
    with jax.named_scope("sum_second"):
        part = scatter(theirs, mine, sums, 0, 5)
        (both,) = call(
            lambda *refs: far_kernel(5, *refs), "for_far", [VMEM],
            [shape(width + TAIL, width, dtype=BF16)], [], (part,), part.size,
        )
        got = flip_chip(both, NEAR)
    with jax.named_scope("outputs"):
        direction, second, subspace = call(
            final_kernel, "outputs", [VMEM] * 7,
            [shape(1, width, width, dtype=BF16), block, shape(4)],
            [], (part, got, wave, inside, first, resid, keep), mine.size, [VMEM, VMEM, SMEM],
        )
    return sigma, direction, second, subspace


def solution(mesh):
    groups, members = mesh.shape["grp"], mesh.shape["op"]
    split = Mesh(mesh.devices.reshape(groups, members // 2, 2), ("grp", "chip", "core"))
    rows = P(("grp", "chip", "core"))
    return jax.shard_map(
        shards,
        mesh=split,
        in_specs=(rows, P("grp"), rows, rows, rows, rows, rows),
        out_specs=(rows, rows, rows, P("grp")),
        check_vma=False,
    )
```

```python
import jax
import jax.numpy as jnp
from jax import lax
from jax.experimental import pallas as pl
from jax.experimental.pallas import tpu as pltpu
from jax.sharding import Mesh
from jax.sharding import PartitionSpec as P

BF16 = jnp.bfloat16
F32 = jnp.float32
TAIL = 16
LIMIT = 36 << 20
LONG = 10**11
TINY = 1e-30
NEAR = 4
GATHER = ((1, 2, 3), (1, 2, 3))
SUMS = ((3, 1, 2), (2, 1, 3))


def each(count, body, carry):
    if count <= 8:
        for j in range(count):
            carry = body(j, carry)
        return carry
    return lax.fori_loop(0, count, body, carry)


def mask_of(size, width):
    rows = lax.broadcasted_iota(jnp.int32, (width, width), 0)
    cols = lax.broadcasted_iota(jnp.int32, (width, width), 1)
    return (rows < size) & (cols < size)


def fold(x):
    return jnp.sum(x, axis=0, keepdims=True)


def eight(x):
    return jnp.sum(x.reshape(-1, 8, x.shape[1]), axis=0)


def at(i, width):
    if isinstance(i, int):
        return slice(i * width, (i + 1) * width)
    return pl.ds(pl.multiple_of(i * width, width), width)


def tail_of(rows):
    pieces = []
    for row in rows:
        rest = row
        for _ in range(3):
            piece = rest.astype(BF16).astype(F32)
            pieces.append(piece)
            rest = rest - piece
    lanes = rows[0].shape[1]
    place = lax.broadcasted_iota(jnp.int32, (TAIL, lanes), 0)
    tail = jnp.zeros((TAIL, lanes), F32)
    for at, piece in enumerate(pieces):
        tail = jnp.where(place == at, piece, tail)
    return tail.astype(BF16)


def rows_of(tail, count):
    wide = tail.astype(F32)
    return [
        (wide[3 * i : 3 * i + 1] + wide[3 * i + 1 : 3 * i + 2]) + wide[3 * i + 2 : 3 * i + 3]
        for i in range(count)
    ]


def total(row):
    return jnp.broadcast_to(jnp.sum(row, axis=1, keepdims=True), row.shape)


def halve(rows):
    while rows.shape[0] > 1:
        half = rows.shape[0] // 2
        rows = rows[:half] + rows[half:]
    return rows


def near_of(orders, core, n):
    if n == 0:
        return 0
    first, second = (order[n - 1] for order in orders)
    return first + (second - first) * core


def apply_blocks(plan, vec, left, right, acc, keep=None):
    terms, nnz = left.shape[0], left.shape[1]
    per = 6 if terms % 6 == 0 else 1

    def step(i, carry):
        items = [(i * per + k, n) for k in range(per) for n in range(nnz)]
        plans = [plan[k, n] for k, n in items]
        prods = [
            jnp.dot(left[k, n], vec[p & 1023], preferred_element_type=F32).astype(BF16)
            for (k, n), p in zip(items, plans)
        ]
        for (k, n), p, prod in zip(items, plans, prods):
            turned = right[k, n]
            if keep is not None:
                turned = turned.T
                keep[k, n] = turned
            acc[p >> 10] += jnp.dot(prod, turned, preferred_element_type=F32)
        return carry

    lax.fori_loop(0, terms // per, step, 0)


def mask_kernel(sizes, block, inside, limits, own):
    own[...] = block[...]
    chips, width = limits.shape[0] // 2, inside.shape[2]
    core, chip = lax.axis_index("core"), lax.axis_index("chip")
    for i in range(2):
        inside[i] = mask_of(sizes[2 * (chip ^ (NEAR * i)) + core], width).astype(F32)

    def size(j, carry):
        for other in range(2):
            row = jnp.full((1, width), sizes[2 * (chip ^ j) + (core ^ other)], jnp.int32)
            limits[pl.ds(other * chips + j, 1)] = row
        return carry

    each(chips, size, 0)


def plan_kernel(src, tgt, plan):
    chips = lax.axis_size("chip")
    chip, core = lax.axis_index("chip"), lax.axis_index("core")

    def place(s):
        return ((s >> 1) ^ chip) + chips * ((s ^ core) & 1)

    plan[...] = place(src[...]) | (place(tgt[...]) << 10)


def pair_kernel(own, far, out):
    out[0:1] = own[...]
    out[1:2] = far[...]


def first_kernel(*refs):
    pieces, ins, outs = refs[: 2 * NEAR], refs[2 * NEAR : 2 * NEAR + 5], refs[2 * NEAR + 5 :]
    plan, limits, left, right, _ = ins
    theirs, acc, wave, flip, sums, rows, places, sem = outs
    span, width = pieces[0].shape[0], pieces[0].shape[2]
    chips = NEAR * span
    core = lax.axis_index("core")
    copy = pltpu.make_async_copy(plan, places, sem)
    copy.start()
    across = lax.broadcasted_iota(jnp.int32, (width, width), 0)
    along = lax.broadcasted_iota(jnp.int32, (width, width), 1)
    acc[...] = jnp.zeros_like(acc)

    for other in range(2):
        for k in range(NEAR):
            piece = pieces[other * NEAR + k]

            def load(i, carry, other=other, k=k, piece=piece):
                rel = other * chips + NEAR * i + near_of(GATHER, core ^ other, k)
                limit = limits[pl.ds(rel, 1)]
                block = jnp.where((across < limit) & (along < limit), piece[i].astype(F32), 0.0)
                wave[rel] = block.astype(BF16)
                rows[rel] = eight(block * block)
                return carry

            each(span, load, 0)
    copy.wait()
    apply_blocks(places, wave, left, right, acc, flip)

    def store(j, ray):
        a, b = acc[j], acc[chips + j]
        theirs[at(j, width)] = b.astype(BF16)
        return ray + eight(wave[j].astype(F32) * a + wave[chips + j].astype(F32) * b)

    ray = fold(each(chips, store, jnp.zeros((8, width), F32)))
    theirs[chips * width :] = tail_of([ray])
    sums[0:1] = ray


def second_kernel(*refs):
    pieces, ins, outs = refs[: 2 * NEAR], refs[2 * NEAR : 2 * NEAR + 6], refs[2 * NEAR + 6 :]
    plan, wave, left, right, first, keep = ins
    theirs, acc, sums, sigma, vec, places, sems = outs
    span, width = pieces[0].shape[0], pieces[0].shape[2]
    chips = NEAR * span
    core = lax.axis_index("core")
    copy = pltpu.make_async_copy(plan, places, sems.at[0])
    result = pltpu.make_async_copy(first, sigma, sems.at[1])
    copy.start()
    result.start()
    acc[...] = jnp.zeros_like(acc)

    for other in range(2):
        for k in range(NEAR):
            piece = pieces[other * NEAR + k]

            def load(i, carry, other=other, k=k, piece=piece):
                vec[other * chips + NEAR * i + near_of(GATHER, core ^ other, k)] = piece[i]
                return carry

            each(span, load, 0)
    copy.wait()
    apply_blocks(places, vec, left, right, acc)

    def store(j, carry):
        cross, square = carry
        a, b = acc[j], acc[chips + j]
        theirs[at(j, width)] = b.astype(BF16)
        cross = cross + eight(wave[j].astype(F32) * a + wave[chips + j].astype(F32) * b)
        square = square + eight(vec[j].astype(F32) * a + vec[chips + j].astype(F32) * b)
        return cross, square

    zero = jnp.zeros((8, width), F32)
    rows = [fold(x) for x in each(chips, store, (zero, zero))]
    rows += [keep[2 + i : 3 + i] for i in range(3)]
    theirs[chips * width :] = tail_of(rows)
    for i, row in enumerate(rows):
        sums[i : i + 1] = row
    result.wait()


def chip_kernel(start, count, mine, got, sums, base, *sends):
    width = mine.shape[2]
    chips, span = mine.shape[0] // 2, base.shape[0]
    core = lax.axis_index("core")
    rows = rows_of(got[chips * width :], count)
    rows = [sums[start + i : start + i + 1] + rows[i] for i in range(count)]
    tail = tail_of(rows)

    def store(i, carry):
        base[i, 0:width] = mine[NEAR * i] + got[at(NEAR * i, width)].astype(F32)
        for n, send in enumerate(sends, 1):
            rel = NEAR * i + near_of(SUMS, core, n)
            send[at(i, width)] = (mine[rel] + got[at(rel, width)].astype(F32)).astype(BF16)
        return carry

    each(span, store, 0)
    for send in sends:
        send[span * width :] = tail
    for i, row in enumerate(rows):
        base[0, width + i : width + i + 1] = row


def near_kernel(count, base, *refs):
    gots, out = refs[:-1], refs[-1]
    span, width = base.shape[0], base.shape[2]
    parts = [[base[0, width + i : width + i + 1] for i in range(count)]]
    came = [rows_of(got[span * width :], count) for got in gots]
    first = lax.axis_index("core") == 0
    for k in range(1, NEAR):
        a, b = (came[order.index(k)] for order in SUMS)
        parts.append([jnp.where(first, x, y) for x, y in zip(a, b)])
    rows = [halve(jnp.concatenate([part[i] for part in parts], axis=0)) for i in range(count)]

    def store(i, carry):
        block = base[i, 0:width]
        for got in gots:
            block = block + got[at(i, width)].astype(F32)
        out[i, 0:width] = block
        for n, row in enumerate(rows):
            out[i, width + n : width + n + 1] = row
        return carry

    each(span, store, 0)


def norm_kernel(rows, wave, base, norms):
    norms[0:1] = total(fold(halve(rows[...])[0]))
    width = wave.shape[2]
    half = wave.shape[0] // 4
    for i in range(2):
        dot = total(fold(base[i, 0:width] * wave[NEAR * i].astype(F32)))
        norms[1 + i : 2 + i] = half * dot / jnp.maximum(total(fold(rows[NEAR * i])), TINY)


def both_kernel(part, wave, norms, out):
    width = part.shape[2]
    rows = [part[0, width : width + 1]]
    for i in range(2):
        own = wave[NEAR * (1 - i)].astype(F32)
        block = part[1 - i, 0:width]
        share = norms[2 - i : 3 - i]
        out[at(i, width)] = (block - share * own).astype(BF16)
        rows.append(share)
    out[2 * width :] = tail_of(rows)


def far_kernel(count, part, out):
    width = part.shape[2]
    out[at(0, width)] = part[1, 0:width].astype(BF16)
    out[width:] = tail_of([part[0, width + i : width + i + 1] for i in range(count)])


def residual_kernel(part, got, wave, inside, precond, far, norms, sigma, resid, send, keep):
    width = part.shape[2]
    ray, *shares = rows_of(got[2 * width :], 3)
    norm, ray = norms[0:1], total(part[0, width : width + 1] + ray)
    energy = ray / norm
    own, other = wave[0].astype(F32), wave[NEAR].astype(F32)
    first = part[0, 0:width] + (got[at(0, width)].astype(F32) + shares[0] * own)
    first = first * inside[0]
    q = precond[0] * (first - energy * own)
    low = q.astype(BF16)
    sigma[0] = first
    resid[0] = q
    send[0] = low
    there = part[1, 0:width] + (got[at(1, width)].astype(F32) + shares[1] * other)
    send[1] = (far[0] * (there * inside[1] - energy * other)).astype(BF16)
    rows = (norm, ray, fold(own * q), fold(low.astype(F32) * first), fold(q * q))
    for i, row in enumerate(rows):
        keep[i : i + 1] = row


def final_kernel(part, got, wave, inside, first, resid, keep, direction, sigma, subspace):
    width = part.shape[2]
    rows = rows_of(got[width:], 5)
    cross, square, inter, mixed, length = (
        total(part[0, width + i : width + i + 1] + rows[i]) for i in range(5)
    )
    norm, ray = keep[0:1], keep[1:2]
    c = inter / norm
    direction[0] = (resid[0] - c * wave[0].astype(F32)).astype(BF16)
    block = part[0, 0:width] + got[at(0, width)].astype(F32)
    sigma[0] = block * inside[0] - c * first[0]
    values = (
        ray,
        cross - c * ray,
        square - c * mixed - c * (cross - c * ray),
        length - 2.0 * c * inter + c * c * norm,
    )
    for i, value in enumerate(values):
        subspace[i] = jnp.max(value / norm)


VMEM = pl.BlockSpec(memory_space=pltpu.VMEM)
SMEM = pl.BlockSpec(memory_space=pltpu.SMEM)
HBM = pl.BlockSpec(memory_space=pl.ANY)


def call(kernel, name, ins, outs, scratch, args, flops, out_specs=None):
    moved = sum(a.size * a.dtype.itemsize for a in args)
    return pl.pallas_call(
        kernel,
        name=name,
        in_specs=ins,
        out_specs=out_specs or [VMEM] * len(outs),
        out_shape=outs,
        scratch_shapes=scratch,
        compiler_params=pltpu.CompilerParams(vmem_limit_bytes=LIMIT),
        cost_estimate=pl.CostEstimate(flops=flops, bytes_accessed=moved, transcendentals=0),
    )(*args)


def shape(*dims, dtype=F32):
    return jax.ShapeDtypeStruct(dims, dtype)


def swap(x):
    return lax.ppermute(x, "core", [(0, 1), (1, 0)])


def flip_chip(x, bits):
    chips = lax.axis_size("chip")
    return lax.ppermute(x, "chip", [(i, i ^ bits) for i in range(chips)])


def flip_near(x, orders, n):
    chips = lax.axis_size("chip")
    pairs = [(2 * i + c, 2 * (i ^ near_of(orders, c, n)) + c) for i in range(chips) for c in range(2)]
    return lax.ppermute(x, ("chip", "core"), pairs)


def gather(block):
    step = NEAR * block.shape[0]
    while step < lax.axis_size("chip"):
        block = jnp.concatenate([block, flip_chip(block, step)], axis=0)
        step *= 2
    pieces = [block] + [flip_near(block, GATHER, n) for n in range(1, NEAR)]
    return pieces + [swap(piece) for piece in pieces]


def scatter(theirs, mine, sums, start, count):
    chips, width = mine.shape[0] // 2, mine.shape[2]
    span, wide = chips // NEAR, width + 8
    sent = [shape(span * width + TAIL, width, dtype=BF16)] * (NEAR - 1)
    base, *sends = call(
        lambda *refs: chip_kernel(start, count, *refs), "chip_sum", [VMEM] * 3,
        [shape(span, wide, width)] + sent, [], (mine, swap(theirs), sums), mine.size,
    )
    gots = [flip_near(send, SUMS, n) for n, send in enumerate(sends, 1)]
    (part,) = call(
        lambda *refs: near_kernel(count, *refs), "near_sum", [VMEM] * NEAR,
        [shape(span, wide, width)], [], (base, *gots), mine.size,
    )
    while span > 2:
        span //= 2
        part = part[:span] + flip_chip(part[span:], NEAR * span)
    return part, base


def shards(state, sector_sizes, left, right, source, target, precond):
    chips = lax.axis_size("chip")
    width = state.shape[1]
    every = 2 * chips
    flops = 4 * left.size * width
    near = [VMEM] * (2 * NEAR)
    block = shape(1, width, width)
    sums_of = shape(8, width)
    after_h = [shape(chips * width + TAIL, width, dtype=BF16), shape(every, width, width)]
    vectors = shape(every, width, width, dtype=BF16)
    places = pltpu.SMEM(source.shape, jnp.int32)

    with jax.named_scope("plan"):
        (plan,) = call(
            plan_kernel, "plan", [VMEM] * 2, [shape(*source.shape, dtype=jnp.int32)], [],
            (source, target), source.size,
        )
        inside, limits, own = call(
            mask_kernel, "masks", [SMEM, VMEM],
            [shape(2, width, width), shape(every, width, dtype=jnp.int32),
             shape(1, width, width, dtype=BF16)],
            [], (sector_sizes, state), LONG,
        )
    with jax.named_scope("gather_state"):
        (pair,) = call(
            pair_kernel, "pair", [VMEM] * 2, [shape(2, width, width, dtype=BF16)], [],
            (own, flip_chip(state, NEAR)), state.size,
        )
        pieces = gather(pair)
        far = flip_chip(precond, NEAR)
    with jax.named_scope("first_sigma"):
        theirs, mine, wave, flip, sums, rows = call(
            first_kernel, "first_sigma", near + [HBM] + [VMEM] * 4,
            after_h + [vectors, shape(*right.shape, dtype=BF16), sums_of, shape(every, 8, width)],
            [places, pltpu.SemaphoreType.DMA],
            (*pieces, plan, limits, left, right, far), flops,
        )
    with jax.named_scope("sum_first"):
        part, base = scatter(theirs, mine, sums, 0, 1)
        (norms,) = call(
            norm_kernel, "norms", [VMEM] * 3, [sums_of], [], (rows, wave, base), rows.size
        )
        (both,) = call(
            both_kernel, "for_far", [VMEM] * 3, [shape(2 * width + TAIL, width, dtype=BF16)], [],
            (part, wave, norms), part.size,
        )
        got = flip_chip(both, NEAR)
    with jax.named_scope("residual"):
        first, resid, send, keep = call(
            residual_kernel, "residual", [VMEM] * 7,
            [block, block, shape(2, width, width, dtype=BF16), sums_of],
            [], (part, got, wave, inside, precond, far, norms), mine.size,
        )
    with jax.named_scope("gather_residual"):
        pieces = gather(send)
    with jax.named_scope("second_sigma"):
        theirs, mine, sums, sigma = call(
            second_kernel, "second_sigma", near + [HBM] + [VMEM] * 5, after_h + [sums_of, block],
            [pltpu.VMEM((every, width, width), BF16), places, pltpu.SemaphoreType.DMA((2,))],
            (*pieces, plan, wave, left, flip, first, keep), flops, [VMEM] * 3 + [HBM],
        )
    with jax.named_scope("sum_second"):
        part, _ = scatter(theirs, mine, sums, 0, 5)
        (both,) = call(
            lambda *refs: far_kernel(5, *refs), "for_far", [VMEM],
            [shape(width + TAIL, width, dtype=BF16)], [], (part,), part.size,
        )
        got = flip_chip(both, NEAR)
    with jax.named_scope("outputs"):
        direction, second, subspace = call(
            final_kernel, "outputs", [VMEM] * 7,
            [shape(1, width, width, dtype=BF16), block, shape(4)],
            [], (part, got, wave, inside, first, resid, keep), mine.size, [VMEM, VMEM, SMEM],
        )
    return sigma, direction, second, subspace


def solution(mesh):
    groups, members = mesh.shape["grp"], mesh.shape["op"]
    split = Mesh(mesh.devices.reshape(groups, members // 2, 2), ("grp", "chip", "core"))
    rows = P(("grp", "chip", "core"))
    return jax.shard_map(
        shards,
        mesh=split,
        in_specs=(rows, P("grp"), rows, rows, rows, rows, rows),
        out_specs=(rows, rows, rows, P("grp")),
        check_vma=False,
    )
```
